128 devices in a mesh: seq: 32 (over z, y, core), chan: 4 (over x).
Axes of the slice: x: 4, y: 4, z: 4, core: 2. Of those that a mesh axis runs over, the one named last changes fastest.
Arguments:
- gate_in: bfloat16 [8192, 8192], P('seq', 'chan'), may hold values from -6 to 6
- key_in: bfloat16 [8192, 8192], P('seq', 'chan'), may hold values from -6 to 6
- value_in: bfloat16 [8192, 8192], P('seq', 'chan'), may hold values from -6 to 6
- conv_out: bfloat16 [8192, 8192], P('seq', 'chan'), may hold values from -6 to 6
- cotangent: bfloat16 [8192, 8192], P('seq', 'chan'), may hold values from -6 to 6
- long_filter: float32 [8192, 8192], P('seq', 'chan'), may hold values from -1.05 to 1.05
- key_taps: float32 [3, 8192], P(None, 'chan'), may hold values from -3 to 3
- value_taps: float32 [3, 8192], P(None, 'chan'), may hold values from -3 to 3
Outputs:
- gate_grad: bfloat16 [8192, 8192], P('seq', 'chan')
- key_grad: bfloat16 [8192, 8192], P('seq', 'chan')
- value_grad: bfloat16 [8192, 8192], P('seq', 'chan')
- filter_grad: float32 [8192, 8192], P('seq', 'chan')
- key_taps_grad: float32 [3, 8192], P(None, 'chan')
- value_taps_grad: float32 [3, 8192], P(None, 'chan')
The draws below stay inside these ranges and needn't reach their ends.
All inputs are finite; a program needn't handle non-finite values.
Results may differ from the reference program's by a relative error of at most 0.0065.
Values may be sent and summed in bfloat16 or wider, within the bound.
No kernel may reach another device: no remote copies, remote signals or barrier semaphores. Data moves between devices by JAX's collectives and lax.ppermute only.
A program may use at most 192 MiB of HBM per device.

```python
import math
import jax
import jax.numpy as jnp
from jax import lax

D = 8192
KS = 3
LENGTH = 8192


def draw_long_filter(key, part):
    key_rate, key_noise = jax.random.split(jax.random.fold_in(key, 7))
    lags = jnp.arange(LENGTH, dtype=jnp.float32)[:, None]
    log_tau = jax.random.uniform(key_rate, (1, D), jnp.float32, math.log(30.0), math.log(4 * LENGTH))
    noise = jax.random.truncated_normal(key_noise, -4.0, 4.0, (LENGTH, D), jnp.float32)
    tau = jnp.exp(log_tau)
    return noise * jnp.exp(-lags / tau) * jnp.sqrt(2.0 / tau)


def shard_levels(key, shape, cuts, least, top_value):
    level = 1.0
    for dim, parts in cuts:
        steps = jax.random.uniform(jax.random.fold_in(jax.random.fold_in(key, 6), dim), (parts,), jnp.float32, least / len(cuts), top_value / len(cuts))
        level = level * jnp.repeat(jnp.exp(steps), shape[dim] // parts).reshape((-1,) + (1,) * (len(shape) - 1 - dim))
    return level


def gaussian(key, shape, spread, bound, shards=(), kind=jnp.bfloat16):
    values = spread * jax.random.normal(key, shape, jnp.float32)
    if shards:
        values = values * shard_levels(key, shape, shards, -0.22, 0.18)
    return jnp.clip(values, -bound, bound).astype(kind)


def setup_inputs(seed: int = 0) -> dict:
    arg_keys = jax.random.split(jax.random.key(seed), 9)
    gate_in = gaussian(arg_keys[0], (LENGTH, D), 1.0, 6.0, ((0, 32), (1, 4)))
    key_in = gaussian(arg_keys[1], (LENGTH, D), 1.0, 6.0, ((0, 32), (1, 4)))
    value_in = gaussian(arg_keys[2], (LENGTH, D), 1.0, 6.0, ((0, 32), (1, 4)))
    conv_out = gaussian(arg_keys[3], (LENGTH, D), 1.0, 6.0, ((0, 32), (1, 4)))
    cotangent = gaussian(arg_keys[4], (LENGTH, D), 1.0, 6.0, ((0, 32), (1, 4)))
    long_filter = draw_long_filter(jax.random.fold_in(arg_keys[8], 71), 0)
    key_taps = gaussian(arg_keys[6], (KS, D), 0.6, 3.0, ((1, 4),), jnp.float32)
    value_taps = gaussian(arg_keys[7], (KS, D), 0.6, 3.0, ((1, 4),), jnp.float32)
    return dict(gate_in=gate_in, key_in=key_in, value_in=value_in, conv_out=conv_out, cotangent=cotangent, long_filter=long_filter, key_taps=key_taps, value_taps=value_taps)


def short_forward(signal, taps):
    count = signal.shape[0]
    padded = jnp.pad(signal, ((KS - 1, 0), (0, 0)))
    total = jnp.zeros_like(signal)
    for offset in range(KS):
        start = KS - 1 - offset
        total = total + taps[offset][None, :] * padded[start:start + count]
    return total

def short_backward(grad, taps):
    count = grad.shape[0]
    padded = jnp.pad(grad, ((0, KS - 1), (0, 0)))
    total = jnp.zeros_like(grad)
    for offset in range(KS):
        total = total + taps[offset][None, :] * padded[offset:offset + count]
    return total

def taps_terms(grad, signal):
    count = signal.shape[0]
    padded = jnp.pad(signal, ((KS - 1, 0), (0, 0)))
    terms = []
    for offset in range(KS):
        start = KS - 1 - offset
        terms.append(lax.optimization_barrier(jnp.sum(grad * padded[start:start + count], axis=0)))
    return jnp.stack(terms, axis=0)

def reference(gate_in, key_in, value_in, conv_out, cotangent, long_filter, key_taps, value_taps):
    key_f = key_in.astype(jnp.float32)
    value_f = value_in.astype(jnp.float32)
    key_short = short_forward(key_f, key_taps)
    value_short = short_forward(value_f, value_taps)
    mixed = (key_short * value_short).astype(jnp.bfloat16)
    cot_f = cotangent.astype(jnp.float32)
    grad_mix = (cot_f * gate_in.astype(jnp.float32)).astype(jnp.bfloat16)
    gate_grad = (cot_f * conv_out.astype(jnp.float32)).astype(jnp.bfloat16)
    length = LENGTH
    total_len = 2 * length
    block = math.gcd(D, 512)
    groups = D // block

    def regroup(array):
        return array.astype(jnp.float32).reshape(length, groups, block).transpose(1, 0, 2)

    def per_block(pieces):
        grad_b, mixed_b, filter_b = pieces
        spec_grad = jnp.fft.rfft(grad_b, n=total_len, axis=0)
        spec_mixed = jnp.fft.rfft(mixed_b, n=total_len, axis=0)
        spec_filter = jnp.fft.rfft(filter_b, n=total_len, axis=0)
        grad_z = jnp.fft.irfft(jnp.conj(spec_filter) * spec_grad, n=total_len, axis=0)[:length]
        grad_h = jnp.fft.irfft(spec_grad * jnp.conj(spec_mixed), n=total_len, axis=0)[:length]
        return (grad_z.astype(jnp.float32), grad_h.astype(jnp.float32))
    grad_z, grad_h = lax.map(per_block, (regroup(grad_mix), regroup(mixed), regroup(long_filter)))
    grad_mixed = grad_z.transpose(1, 0, 2).reshape(length, D)
    raw_filter_grad = grad_h.transpose(1, 0, 2).reshape(length, D)
    grad_key_short = grad_mixed * value_short
    grad_value_short = grad_mixed * key_short
    key_grad = short_backward(grad_key_short, key_taps).astype(jnp.bfloat16)
    value_grad = short_backward(grad_value_short, value_taps).astype(jnp.bfloat16)
    key_taps_grad = taps_terms(grad_key_short, key_f)
    value_taps_grad = taps_terms(grad_value_short, value_f)
    filter_rms = jnp.sqrt(jnp.sum(raw_filter_grad * raw_filter_grad) / (length * D) + 1e-06)
    filter_grad = raw_filter_grad * jnp.minimum(1.0, 1.0 / filter_rms)
    return (gate_grad, key_grad, value_grad, filter_grad, key_taps_grad, value_taps_grad)
```

```python
import functools
import math

import jax
import jax.numpy as jnp
import numpy as np
from jax import lax
from jax.experimental import pallas as pl
from jax.experimental.pallas import tpu as pltpu
from jax.sharding import PartitionSpec as P

BF = jnp.bfloat16
F32 = jnp.float32
HALF = 64
MIB = 1 << 20


def transform_tables(parts, rows):
    length = parts * rows
    mid = rows // 2
    p = np.arange(parts)
    k = np.arange(parts)
    step = math.pi / (2 * length)
    angle = ((rows * p[None, :] * (4 * k[:, None] + 1)) % (4 * length)) * step
    first = np.stack([np.cos(angle), -np.sin(angle)], 1)
    forward = np.einsum("kcp,rs->kcrps", first, np.eye(8)).reshape(parts * 16, parts * 8)
    backward = forward.T / length
    angle = ((np.arange(rows)[None, :] * (4 * k[:, None] + 1)) % (4 * length)) * step
    factors = np.stack([np.cos(angle), np.sin(angle)], 1).astype(np.float32)
    r, j = np.arange(mid)[:, None], np.arange(mid)[None, :]
    second = []
    for odd in (0, 1):
        turn = (((2 * j + odd) * r) % rows) * (2 * math.pi / rows)
        cos, sin = np.cos(turn), np.sin(turn)
        second.append(np.block([[cos, -sin], [sin, cos]]))
    as_bf = lambda x: x.astype(np.float32).astype(jnp.bfloat16)
    second = np.stack(second)
    return as_bf(forward), as_bf(second), as_bf(second.transpose(0, 2, 1)), as_bf(backward), factors


def low_lanes(shape):
    return (lax.broadcasted_iota(jnp.int32, shape, len(shape) - 1) % 128) < HALF


def swap_halves(x):
    return pltpu.roll(x, HALF, axis=x.ndim - 1)


def spectral_kernel(recv, m1, w, wi, m2, factors, gz_out, gh_out, y, u, acc):
    parts, chans, rows = recv.shape
    chans //= 3
    mid = rows // 2
    group = 16

    @pl.loop(0, 3 * chans // 16, unroll=2)
    def _(i):
        base = pl.multiple_of(16 * i, 16)
        x = recv[:, pl.ds(base, 16), :].astype(F32)
        out = []
        for q in range(2):
            xq = x[:, 8 * q : 8 * q + 8, :].reshape(parts * 8, rows).astype(BF)
            out.append(jnp.dot(m1[...], xq, preferred_element_type=F32))
        for k in range(parts):
            c, s = factors[k, 0:1, :], factors[k, 1:2, :]
            sums, gaps = [], []
            for q in range(2):
                re, im = out[q][16 * k : 16 * k + 8], out[q][16 * k + 8 : 16 * k + 16]
                turned = (re * c + im * s, im * c - re * s)
                sums.append(jnp.concatenate([t[:, :mid] + t[:, mid:] for t in turned], axis=1))
                gaps.append(jnp.concatenate([t[:, :mid] - t[:, mid:] for t in turned], axis=1))
            y[0, k, pl.ds(base, 16), :] = jnp.concatenate(sums, axis=0).astype(BF)
            y[1, k, pl.ds(base, 16), :] = jnp.concatenate(gaps, axis=0).astype(BF)

    @pl.loop(0, parts // group)
    def _(kk):
        backs = []
        for odd in range(2):
            lines = y[odd, pl.ds(group * kk, group)].reshape(group * 3 * chans, rows)
            spec = jnp.dot(lines, w[odd], preferred_element_type=F32)
            products = []
            for n in range(group):
                at = 3 * chans * n
                grad = spec[at + 2 * chans : at + 3 * chans]
                gr, gi = grad[:, :mid], grad[:, mid:]
                for h in range(2):
                    part = spec[at + h * chans : at + (h + 1) * chans]
                    sr, si = part[:, :mid], part[:, mid:]
                    products.append(jnp.concatenate([sr * gr + si * gi, sr * gi - si * gr], axis=1))
            product = jnp.concatenate(products, axis=0).astype(BF)
            backs.append(jnp.dot(product, wi[odd], preferred_element_type=F32))
        for h, back in enumerate((backs[0] + backs[1], backs[0] - backs[1])):
            cols = slice(mid * h, mid * h + mid)
            for n in range(group):
                k = group * kk + n
                c, s = factors[k, 0:1, cols], factors[k, 1:2, cols]
                lines = back[2 * chans * n : 2 * chans * (n + 1)]
                re, im = lines[:, :mid], lines[:, mid:]
                u[2 * k, :, cols] = (re * c - im * s).astype(BF)
                u[2 * k + 1, :, cols] = (im * c + re * s).astype(BF)

    acc[...] = jnp.zeros_like(acc)

    def backward(base):
        piece = u[:, pl.ds(base, 16), :].astype(F32)
        outs = []
        for q in range(2):
            v = piece[:, 8 * q : 8 * q + 8, :].reshape(parts * 16, rows).astype(BF)
            out = jnp.dot(m2[...], v, preferred_element_type=F32)
            outs.append(out.reshape(parts, 8, rows))
        return jnp.concatenate(outs, axis=1)

    @pl.loop(0, chans // 16, unroll=2)
    def _(i):
        base = pl.multiple_of(16 * i, 16)
        grad = backward(base)
        for h in range(2):
            gz_out[:, pl.ds(chans * h + base, 16), :] = grad[:, :, mid * h : mid * h + mid].astype(BF)

    @pl.loop(0, chans // 16, unroll=2)
    def _(i):
        base = pl.multiple_of(16 * i, 16)
        grad = backward(chans + base)
        for h in range(2):
            gh_out[:, pl.ds(chans * h + base, 16), :] = grad[:, :, mid * h : mid * h + mid].astype(BF)
        acc[...] += jnp.sum((grad * grad).reshape(parts * 2, 8, rows), axis=0)

    total = jnp.sum(jnp.sum(acc[...], axis=0, keepdims=True), axis=1, keepdims=True)
    coarse = total.astype(BF).astype(F32)
    fine = (total - coarse).astype(BF).astype(F32)
    row = lax.broadcasted_iota(jnp.int32, (16, 128), 0)
    sums = jnp.where(row == 2, coarse, jnp.where(row == 3, fine, 0.0))
    lane = lax.broadcasted_iota(jnp.int32, (16, mid), 1)
    pick = jnp.where((lane == lax.broadcasted_iota(jnp.int32, (16, mid), 0)) & (lane < 2), 1.0, 0.0).astype(BF)
    firsts = gz_out[:, :chans, :].reshape(parts * chans, mid)
    edges = lax.dot_general(pick, firsts, (((1,), (1,)), ((), ())), preferred_element_type=F32)
    for p in range(parts):
        after = jnp.zeros((16, 128), F32)
        if p + 1 < parts:
            at = (p + 1) // 2 * 128
            after = edges[:, at : at + 128]
            if (p + 1) % 2:
                after = swap_halves(after)
        gz_out[p, 2 * chans : 2 * chans + 16, :] = jnp.where(row < 2, after, sums).astype(BF)


def spectral(recv, parts, rows):
    tables = transform_tables(parts, rows)
    chans = recv.shape[1] // 3
    mid = rows // 2
    vmem = pl.BlockSpec(memory_space=pltpu.VMEM)
    flops = 2 * parts * parts * 16 * 8 * rows * chans // 8 * 5 + 2 * parts * rows * rows * chans * 10
    return pl.pallas_call(
        spectral_kernel,
        out_shape=(
            jax.ShapeDtypeStruct((parts, 2 * chans + 16, mid), BF),
            jax.ShapeDtypeStruct((parts, 2 * chans, mid), BF),
        ),
        in_specs=[vmem] * 6,
        out_specs=(vmem, vmem),
        scratch_shapes=[
            pltpu.VMEM((2, parts, 3 * chans, rows), BF),
            pltpu.VMEM((2 * parts, 2 * chans, rows), BF),
            pltpu.VMEM((8, rows), F32),
        ],
        compiler_params=pltpu.CompilerParams(vmem_limit_bytes=60 * MIB),
        cost_estimate=pl.CostEstimate(flops=flops, bytes_accessed=7 * MIB, transcendentals=0),
        name="spectral",
    )(recv, *[jnp.asarray(x) for x in tables])


def row_index(x):
    return lax.broadcasted_iota(jnp.int32, x.shape, 0)


def delayed(x, before):
    row = row_index(x)
    one = jnp.where(row == 0, before[1:2], pltpu.roll(x, 1, axis=0))
    two = jnp.where(row == 0, before[0:1], jnp.where(row == 1, before[1:2], pltpu.roll(x, 2, axis=0)))
    return one, two


def prepare_kernel(cot, gate, key, value, filt, key_taps, value_taps, before, send):
    rows, lanes = cot.shape
    mid = rows // 2
    grad = cot[...].astype(F32) * gate[...].astype(F32)
    kf, vf = key[...].astype(F32), value[...].astype(F32)
    edge = before[...].astype(F32)
    k1, k2 = delayed(kf, edge[0:2])
    v1, v2 = delayed(vf, edge[2:4])
    kt, vt = key_taps[...], value_taps[...]
    key_short = kt[0:1] * kf + kt[1:2] * k1 + kt[2:3] * k2
    value_short = vt[0:1] * vf + vt[1:2] * v1 + vt[2:3] * v2
    mixed = key_short * value_short
    for j in range(lanes // 128):
        cols = slice(128 * j, 128 * j + 128)
        for n, x in enumerate((filt[:, cols], mixed[:, cols], grad[:, cols])):
            x = x.astype(BF)
            turned = jnp.concatenate([x[:mid].T, x[mid:].T], axis=1)
            send[2 * j, HALF * n : HALF * n + HALF, :] = turned[:HALF]
            send[2 * j + 1, HALF * n : HALF * n + HALF, :] = turned[HALF:]


def column_call(kernel, name, ins, outs, lanes, columns):
    def spec(shape):
        if len(shape) == 3:
            return pl.BlockSpec((shape[0] * lanes // columns,) + shape[1:], lambda i: (i, 0, 0))
        return pl.BlockSpec((shape[0], lanes), lambda i: (0, i))

    size = sum(math.prod(a.shape) * a.dtype.itemsize for a in list(ins) + list(outs))
    return pl.pallas_call(
        kernel,
        grid=(columns // lanes,),
        in_specs=[spec(a.shape) for a in ins],
        out_specs=[spec(a.shape) for a in outs],
        out_shape=outs,
        compiler_params=pltpu.CompilerParams(vmem_limit_bytes=60 * MIB),
        cost_estimate=pl.CostEstimate(flops=size, bytes_accessed=size, transcendentals=0),
        name=name,
    )(*ins)


def gate_kernel(cot, conv, out):
    out[...] = (cot[...].astype(F32) * conv[...].astype(F32)).astype(BF)


def unpack(first, second):
    pairs = [jnp.concatenate([x[at : at + HALF] for x in (first, second)], axis=0) for at in (0, HALF)]
    return jnp.concatenate([pair.T for pair in pairs], axis=0).astype(F32)


def finish_kernel(grads, key, value, key_taps, value_taps, before, after, key_out, value_out, taps_out):
    rows, lanes = key.shape
    pieces, edges = [], []
    for j in range(lanes // 128):
        first, second = grads[2 * j], grads[2 * j + 1]
        pieces.append(unpack(first, second))
        edge = [x[2 * HALF : 2 * HALF + 16].astype(F32) for x in (first, second)]
        edges.append(jnp.where(low_lanes((16, 128)), edge[0], swap_halves(edge[1])))
    gz = jnp.concatenate(pieces, axis=1)
    edge = jnp.concatenate(edges, axis=1)
    next0, next1 = edge[0:1], edge[1:2]
    kf, vf = key[...].astype(F32), value[...].astype(F32)
    prev, post = before[...].astype(F32), after[...].astype(F32)
    k1, k2 = delayed(kf, prev[0:2])
    v1, v2 = delayed(vf, prev[2:4])
    kt, vt = key_taps[...], value_taps[...]
    row = row_index(kf)

    def short(taps, x0, x1, x2):
        return taps[0:1] * x0 + taps[1:2] * x1 + taps[2:3] * x2

    def beyond(taps, x, edge):
        last, prior = x[rows - 1 : rows], x[rows - 2 : rows - 1]
        return short(taps, edge[0:1], last, prior), short(taps, edge[1:2], edge[0:1], last)

    def backward(taps, grad, grad0, grad1):
        one = jnp.where(row == rows - 1, grad0, pltpu.roll(grad, rows - 1, axis=0))
        two = jnp.where(row == rows - 2, grad0, jnp.where(row == rows - 1, grad1, pltpu.roll(grad, rows - 2, axis=0)))
        return short(taps, grad, one, two)

    key_short, value_short = short(kt, kf, k1, k2), short(vt, vf, v1, v2)
    key_a, key_b = beyond(kt, kf, post[0:2])
    value_a, value_b = beyond(vt, vf, post[2:4])
    grad_key, grad_value = gz * value_short, gz * key_short
    key_out[...] = backward(kt, grad_key, next0 * value_a, next1 * value_b).astype(BF)
    value_out[...] = backward(vt, grad_value, next0 * key_a, next1 * key_b).astype(BF)
    sums = [jnp.sum(grad_key * x, axis=0, keepdims=True) for x in (kf, k1, k2)]
    sums += [jnp.sum(grad_value * x, axis=0, keepdims=True) for x in (vf, v1, v2)]
    taps_out[...] = jnp.concatenate(sums + [jnp.zeros((2, lanes), F32)], axis=0)


def clip_kernel(grads, scale, out):
    factor = scale[0:1, 0:1]
    for j in range(out.shape[1] // 128):
        out[:, 128 * j : 128 * j + 128] = unpack(grads[2 * j], grads[2 * j + 1]) * factor


def clip(grads, scale, rows, columns, lanes):
    per = grads.shape[0] * lanes // columns
    return pl.pallas_call(
        clip_kernel,
        grid=(columns // lanes,),
        in_specs=[
            pl.BlockSpec((per,) + grads.shape[1:], lambda i: (i, 0, 0)),
            pl.BlockSpec((1, 1), lambda i: (0, 0)),
        ],
        out_specs=pl.BlockSpec((rows, lanes), lambda i: (0, i)),
        out_shape=jax.ShapeDtypeStruct((rows, columns), F32),
        compiler_params=pltpu.CompilerParams(vmem_limit_bytes=60 * MIB),
        cost_estimate=pl.CostEstimate(flops=rows * columns * 4, bytes_accessed=rows * columns * 6, transcendentals=0),
        name="clip",
    )(grads, scale)


def tree_sum(x, axis, size):
    step = 1
    while step < size:
        x = x + lax.ppermute(x, axis, [(i, i ^ step) for i in range(size)])
        step *= 2
    return x


def shards(gate_in, key_in, value_in, conv_out, cotangent, long_filter, key_taps, value_taps, *, parts, others):
    rows, columns = key_in.shape
    shape = jax.ShapeDtypeStruct
    tails = jnp.concatenate([key_in[-2:], value_in[-2:]], axis=0)
    heads = jnp.concatenate([key_in[:2], value_in[:2]], axis=0)
    before = lax.ppermute(tails, "seq", [(i, i + 1) for i in range(parts - 1)])
    after = lax.ppermute(heads, "seq", [(i + 1, i) for i in range(parts - 1)])
    before, after = lax.optimization_barrier((before, after))
    (send,) = column_call(
        prepare_kernel,
        "prepare",
        (cotangent, gate_in, key_in, value_in, long_filter, key_taps, value_taps, before),
        (shape((parts, 3 * HALF, rows), BF),),
        1024,
        columns,
    )
    recv = lax.all_to_all(send, "seq", 0, 0)
    (gate_grad,) = column_call(gate_kernel, "gate", (cotangent, conv_out), (shape((rows, columns), BF),), 1024, columns)
    recv, gate_grad = lax.optimization_barrier((recv, gate_grad))
    gz_send, gh_send = spectral(recv, parts, rows)
    gz_recv = lax.all_to_all(gz_send, "seq", 0, 0)
    gz_recv, gh_send = lax.optimization_barrier((gz_recv, gh_send))
    gh_recv = lax.all_to_all(gh_send, "seq", 0, 0)
    squares = jnp.sum(gz_recv[:, 2 * HALF + 2 : 2 * HALF + 4, 0].astype(F32)).reshape(1, 1)
    total = tree_sum(squares, "chan", others)
    count = rows * columns * parts * others
    scale = jnp.minimum(1.0, 1.0 / jnp.sqrt(total / count + 1e-6))
    key_grad, value_grad, taps = column_call(
        finish_kernel,
        "finish",
        (gz_recv, key_in, value_in, key_taps, value_taps, before, after),
        (shape((rows, columns), BF), shape((rows, columns), BF), shape((8, columns), F32)),
        512,
        columns,
    )
    taps = tree_sum(taps, "seq", parts)
    filter_grad = clip(gh_recv, scale, rows, columns, 1024)
    return (gate_grad, key_grad, value_grad, filter_grad, taps[0:3], taps[3:6])


def solution(mesh):
    blocks, vectors = P("seq", "chan"), P(None, "chan")
    return jax.shard_map(
        functools.partial(shards, parts=mesh.shape["seq"], others=mesh.shape["chan"]),
        mesh=mesh,
        in_specs=(blocks,) * 6 + (vectors,) * 2,
        out_specs=(blocks,) * 4 + (vectors,) * 2,
        check_vma=False,
    )
```

```python
import functools
import math

import jax
import jax.numpy as jnp
import numpy as np
from jax import lax
from jax.experimental import pallas as pl
from jax.experimental.pallas import tpu as pltpu
from jax.sharding import PartitionSpec as P

BF = jnp.bfloat16
F32 = jnp.float32
HALF = 64
MIB = 1 << 20
SPECTRAL_LIMIT = 62
LATE_LIMIT = 24


def transform_tables(parts, rows):
    length = parts * rows
    mid = rows // 2
    p = np.arange(parts)
    k = np.arange(parts)
    step = math.pi / (2 * length)
    angle = ((rows * p[None, :] * (4 * k[:, None] + 1)) % (4 * length)) * step
    first = np.stack([np.cos(angle), -np.sin(angle)], 1)
    forward = np.einsum("kcp,rs->kcrps", first, np.eye(8)).reshape(parts * 16, parts * 8)
    backward = forward.T / length
    angle = ((np.arange(rows)[None, :] * (4 * k[:, None] + 1)) % (4 * length)) * step
    factors = np.stack([np.cos(angle), np.sin(angle)], 1).astype(np.float32)
    r, j = np.arange(mid)[:, None], np.arange(mid)[None, :]
    second = []
    for odd in (0, 1):
        turn = (((2 * j + odd) * r) % rows) * (2 * math.pi / rows)
        cos, sin = np.cos(turn), np.sin(turn)
        second.append(np.block([[cos, -sin], [sin, cos]]))
    as_bf = lambda x: x.astype(np.float32).astype(jnp.bfloat16)
    second = np.stack(second)
    return as_bf(forward), as_bf(second), as_bf(second.transpose(0, 2, 1)), as_bf(backward), factors


def low_lanes(shape):
    return (lax.broadcasted_iota(jnp.int32, shape, len(shape) - 1) % 128) < HALF


def swap_halves(x):
    return pltpu.roll(x, HALF, axis=x.ndim - 1)


def spectral_kernel(recv, m1, w, wi, m2, factors, gz_out, gh_out, x_v, gz_v, gh_v, y, u, acc, in_sems, out_sems):
    parts, chans, rows = recv.shape
    chans //= 3
    mid = rows // 2
    group = 16
    pieces = 3 * chans // 32

    def fetch(i):
        at = pl.ds(32 * i, 32)
        return pltpu.make_async_copy(recv.at[:, at, :], x_v.at[:, at, :], in_sems.at[i])

    for i in range(pieces):
        fetch(i).start()

    def forward(base):
        x = x_v[:, pl.ds(base, 16), :].astype(F32)
        out = []
        for q in range(2):
            xq = x[:, 8 * q : 8 * q + 8, :].reshape(parts * 8, rows).astype(BF)
            out.append(jnp.dot(m1[...], xq, preferred_element_type=F32))
        for k in range(parts):
            c, s = factors[k, 0:1, :], factors[k, 1:2, :]
            sums, gaps = [], []
            for q in range(2):
                re, im = out[q][16 * k : 16 * k + 8], out[q][16 * k + 8 : 16 * k + 16]
                turned = (re * c + im * s, im * c - re * s)
                sums.append(jnp.concatenate([t[:, :mid] + t[:, mid:] for t in turned], axis=1))
                gaps.append(jnp.concatenate([t[:, :mid] - t[:, mid:] for t in turned], axis=1))
            y[0, k, pl.ds(base, 16), :] = jnp.concatenate(sums, axis=0).astype(BF)
            y[1, k, pl.ds(base, 16), :] = jnp.concatenate(gaps, axis=0).astype(BF)

    @pl.loop(0, pieces)
    def _(i):
        fetch(i).wait()
        for q in range(2):
            forward(pl.multiple_of(32 * i + 16 * q, 16))

    @pl.loop(0, parts // group)
    def _(kk):
        backs = []
        for odd in range(2):
            lines = y[odd, pl.ds(group * kk, group)].reshape(group * 3 * chans, rows)
            spec = jnp.dot(lines, w[odd], preferred_element_type=F32)
            products = []
            for n in range(group):
                at = 3 * chans * n
                grad = spec[at + 2 * chans : at + 3 * chans]
                gr, gi = grad[:, :mid], grad[:, mid:]
                for h in range(2):
                    part = spec[at + h * chans : at + (h + 1) * chans]
                    sr, si = part[:, :mid], part[:, mid:]
                    products.append(jnp.concatenate([sr * gr + si * gi, sr * gi - si * gr], axis=1))
            product = jnp.concatenate(products, axis=0).astype(BF)
            backs.append(jnp.dot(product, wi[odd], preferred_element_type=F32))
        for h, back in enumerate((backs[0] + backs[1], backs[0] - backs[1])):
            cols = slice(mid * h, mid * h + mid)
            for n in range(group):
                k = group * kk + n
                c, s = factors[k, 0:1, cols], factors[k, 1:2, cols]
                lines = back[2 * chans * n : 2 * chans * (n + 1)]
                re, im = lines[:, :mid], lines[:, mid:]
                u[2 * k, :, cols] = (re * c - im * s).astype(BF)
                u[2 * k + 1, :, cols] = (im * c + re * s).astype(BF)

    acc[...] = jnp.zeros_like(acc)

    def backward(base):
        piece = u[:, pl.ds(base, 16), :].astype(F32)
        outs = []
        for q in range(2):
            v = piece[:, 8 * q : 8 * q + 8, :].reshape(parts * 16, rows).astype(BF)
            out = jnp.dot(m2[...], v, preferred_element_type=F32)
            outs.append(out.reshape(parts, 8, rows))
        return jnp.concatenate(outs, axis=1)

    tiles = chans // 16

    def store(target, scratch, first, row):
        at = pl.ds(pl.multiple_of(row, 16), 16)
        return pltpu.make_async_copy(scratch.at[:, at, :], target.at[:, at, :], out_sems.at[first])

    @pl.loop(0, tiles // 2)
    def _(i):
        for q in range(2):
            base = pl.multiple_of(32 * i + 16 * q, 16)
            grad = backward(chans + base)
            for h in range(2):
                gh_v[:, pl.ds(chans * h + base, 16), :] = grad[:, :, mid * h : mid * h + mid].astype(BF)
                store(gh_out, gh_v, tiles * h + 2 * i + q, chans * h + base).start()
            acc[...] += jnp.sum((grad * grad).reshape(parts * 2, 8, rows), axis=0)

    @pl.loop(0, tiles // 2)
    def _(i):
        for q in range(2):
            base = pl.multiple_of(32 * i + 16 * q, 16)
            grad = backward(base)
            for h in range(2):
                gz_v[:, pl.ds(chans * h + base, 16), :] = grad[:, :, mid * h : mid * h + mid].astype(BF)
                store(gz_out, gz_v, 2 * tiles + tiles * h + 2 * i + q, chans * h + base).start()

    total = jnp.sum(jnp.sum(acc[...], axis=0, keepdims=True), axis=1, keepdims=True)
    coarse = total.astype(BF).astype(F32)
    fine = (total - coarse).astype(BF).astype(F32)
    row = lax.broadcasted_iota(jnp.int32, (16, 128), 0)
    sums = jnp.where(row == 2, coarse, jnp.where(row == 3, fine, 0.0))
    lane = lax.broadcasted_iota(jnp.int32, (16, mid), 1)
    pick = jnp.where((lane == lax.broadcasted_iota(jnp.int32, (16, mid), 0)) & (lane < 2), 1.0, 0.0).astype(BF)
    firsts = gz_v[:, :chans, :].reshape(parts * chans, mid)
    edges = lax.dot_general(pick, firsts, (((1,), (1,)), ((), ())), preferred_element_type=F32)
    for p in range(parts):
        after = jnp.zeros((16, 128), F32)
        if p + 1 < parts:
            at = (p + 1) // 2 * 128
            after = edges[:, at : at + 128]
            if (p + 1) % 2:
                after = swap_halves(after)
        gz_v[p, 2 * chans : 2 * chans + 16, :] = jnp.where(row < 2, after, sums).astype(BF)
    store(gz_out, gz_v, 4 * tiles, 2 * chans).start()
    for n in range(2 * tiles):
        store(gh_out, gh_v, n, 16 * n).wait()
        store(gz_out, gz_v, 2 * tiles + n, 16 * n).wait()
    store(gz_out, gz_v, 4 * tiles, 2 * chans).wait()


def spectral(recv, parts, rows):
    tables = transform_tables(parts, rows)
    chans = recv.shape[1] // 3
    mid = rows // 2
    vmem = pl.BlockSpec(memory_space=pltpu.VMEM)
    anywhere = pl.BlockSpec(memory_space=pl.ANY)
    flops = 2 * parts * parts * 16 * 8 * rows * chans // 8 * 5 + 2 * parts * rows * rows * chans * 10
    return pl.pallas_call(
        spectral_kernel,
        out_shape=(
            jax.ShapeDtypeStruct((parts, 2 * chans + 16, mid), BF),
            jax.ShapeDtypeStruct((parts, 2 * chans, mid), BF),
        ),
        in_specs=[anywhere] + [vmem] * 5,
        out_specs=(anywhere, anywhere),
        scratch_shapes=[
            pltpu.VMEM(recv.shape, BF),
            pltpu.VMEM((parts, 2 * chans + 16, mid), BF),
            pltpu.VMEM((parts, 2 * chans, mid), BF),
            pltpu.VMEM((2, parts, 3 * chans, rows), BF),
            pltpu.VMEM((2 * parts, 2 * chans, rows), BF),
            pltpu.VMEM((8, rows), F32),
            pltpu.SemaphoreType.DMA((3 * chans // 32,)),
            pltpu.SemaphoreType.DMA((4 * (chans // 16) + 1,)),
        ],
        compiler_params=pltpu.CompilerParams(vmem_limit_bytes=SPECTRAL_LIMIT * MIB),
        cost_estimate=pl.CostEstimate(flops=flops, bytes_accessed=7 * MIB, transcendentals=0),
        name="spectral",
    )(recv, *[jnp.asarray(x) for x in tables])


def row_index(x):
    return lax.broadcasted_iota(jnp.int32, x.shape, 0)


def with_top(x, rows):
    top = x[:8]
    for n, line in enumerate(rows):
        top = jnp.where(row_index(top) == n, line, top)
    return jnp.concatenate([top, x[8:]], axis=0)


def with_bottom(x, rows):
    end = x.shape[0]
    bottom = x[end - 8 :]
    for n, line in enumerate(rows):
        bottom = jnp.where(row_index(bottom) == 8 - len(rows) + n, line, bottom)
    return jnp.concatenate([x[: end - 8], bottom], axis=0)


def delayed(x, before):
    first, second = before[0:1], before[1:2]
    one = with_top(pltpu.roll(x, 1, axis=0), [second])
    two = with_top(pltpu.roll(x, 2, axis=0), [first, second])
    return one, two


def stream(body, name, ins, smalls, outs, parts_of, chunks, limit, alias=None):
    def size(shape):
        return (shape[0] // chunks,) + tuple(shape[1:]) if len(shape) == 3 else (shape[0], shape[1] // chunks)

    def window(ref, c, rows=None):
        if len(ref.shape) == 2:
            per = ref.shape[1] // chunks
            return ref.at[:, pl.ds(pl.multiple_of(c * per, 128), per)]
        per = ref.shape[0] // chunks
        at = ref.at[pl.ds(c * per, per)]
        return at if rows is None else ref.at[pl.ds(c * per, per), pl.ds(rows[0], rows[1]), :]

    extra = [] if alias is None else [alias]
    n_in, n_small, n_out, n_part = len(ins), len(smalls), len(outs), len(parts_of)

    def kernel(*refs):
        refs = list(refs)
        take = lambda n: [refs.pop(0) for _ in range(n)]
        in_refs, small_refs, _, out_refs = take(n_in), take(n_small), take(len(extra)), take(n_out)
        in_v, small_v, out_v = take(n_in), take(n_small), take(n_part)
        in_sems, small_sems, out_sems = refs

        def fetch(n, c):
            return pltpu.make_async_copy(window(in_refs[n], c), in_v[n].at[c], in_sems.at[n, c])

        def store(n, c):
            index, rows = parts_of[n]
            return pltpu.make_async_copy(out_v[n].at[c], window(out_refs[index], c, rows), out_sems.at[n, c])

        smalls_in = [pltpu.make_async_copy(small_refs[n], small_v[n], small_sems.at[n]) for n in range(n_small)]
        for copy in smalls_in:
            copy.start()
        for c in range(chunks):
            for n in range(n_in):
                fetch(n, c).start()
        for copy in smalls_in:
            copy.wait()

        @pl.loop(0, chunks)
        def _(c):
            for n in range(n_in):
                fetch(n, c).wait()
            body(c, [v.at[c] for v in in_v], small_v, [v.at[c] for v in out_v])
            for n in range(n_part):
                store(n, c).start()

        for c in range(chunks):
            for n in range(n_part):
                store(n, c).wait()

    scratch = [pltpu.VMEM((chunks,) + size(a.shape), a.dtype) for a in ins]
    scratch += [pltpu.VMEM(a.shape, a.dtype) for a in smalls]
    for index, rows in parts_of:
        shape = size(outs[index].shape)
        if rows is not None:
            shape = (shape[0], rows[1], shape[2])
        scratch.append(pltpu.VMEM((chunks,) + shape, outs[index].dtype))
    scratch += [pltpu.SemaphoreType.DMA((n_in, chunks)), pltpu.SemaphoreType.DMA((max(n_small, 1),)), pltpu.SemaphoreType.DMA((n_part, chunks))]
    total = sum(math.prod(a.shape) * a.dtype.itemsize for a in list(ins) + list(outs))
    anywhere = pl.BlockSpec(memory_space=pl.ANY)
    return pl.pallas_call(
        kernel,
        in_specs=[anywhere] * (n_in + n_small + len(extra)),
        out_specs=[anywhere] * n_out,
        out_shape=outs,
        scratch_shapes=scratch,
        input_output_aliases={} if alias is None else {n_in + n_small: 0},
        compiler_params=pltpu.CompilerParams(vmem_limit_bytes=limit * MIB),
        cost_estimate=pl.CostEstimate(flops=total, bytes_accessed=total, transcendentals=0),
        name=name,
    )(*ins, *smalls, *extra)


def columns_of(ref, c, lanes):
    return ref[:, pl.ds(pl.multiple_of(c * lanes, 128), lanes)]


def short(taps, x0, x1, x2):
    return taps[0:1] * x0 + taps[1:2] * x1 + taps[2:3] * x2


def turn_out(x, out):
    rows, lanes = x.shape
    mid = rows // 2
    x = x.astype(BF)
    for j in range(lanes // 128):
        cols = slice(128 * j, 128 * j + 128)
        turned = jnp.concatenate([x[:mid, cols].T, x[mid:, cols].T], axis=1)
        out[2 * j] = turned[:HALF]
        out[2 * j + 1] = turned[HALF:]


def known_body(c, ins, smalls, outs):
    cot, gate, filt = ins
    turn_out(filt[...], outs[0])
    turn_out(cot[...].astype(F32) * gate[...].astype(F32), outs[1])


def mixed_body(c, ins, smalls, outs):
    kf, vf = (x[...].astype(F32) for x in ins)
    kt, vt, before = (columns_of(x, c, kf.shape[1]).astype(F32) for x in smalls)
    key_short = short(kt, kf, *delayed(kf, before[0:2]))
    value_short = short(vt, vf, *delayed(vf, before[2:4]))
    turn_out(key_short * value_short, outs[0])


def gate_body(c, ins, smalls, outs):
    cot, conv = ins
    outs[0][...] = (cot[...].astype(F32) * conv[...].astype(F32)).astype(BF)


def turn_in(blocks):
    tiles = []
    for j in range(blocks.shape[0] // 2):
        pair = (blocks[2 * j], blocks[2 * j + 1])
        halves = [jnp.concatenate([x[at : at + HALF] for x in pair], axis=0).T for at in (0, HALF)]
        tiles.append(jnp.concatenate(halves, axis=0))
    return jnp.concatenate(tiles, axis=1).astype(F32)


def taps_body(c, ins, smalls, outs):
    grads, key, value = ins
    gz = turn_in(grads)
    kf, vf = key[...].astype(F32), value[...].astype(F32)
    kt, vt, before = (columns_of(x, c, kf.shape[1]).astype(F32) for x in smalls)
    ks, vs = (kf,) + delayed(kf, before[0:2]), (vf,) + delayed(vf, before[2:4])
    grad_key, grad_value = gz * short(vt, *vs), gz * short(kt, *ks)
    sums = [jnp.sum(grad_key * x, axis=0, keepdims=True) for x in ks]
    sums += [jnp.sum(grad_value * x, axis=0, keepdims=True) for x in vs]
    outs[0][...] = jnp.concatenate(sums + [jnp.zeros((2, kf.shape[1]), F32)], axis=0)


def inputs_body(c, ins, smalls, outs):
    grads, key, value = ins
    rows, lanes = key.shape
    gz = turn_in(grads)
    kf, vf = key[...].astype(F32), value[...].astype(F32)
    kt, vt, before, after = (columns_of(x, c, lanes).astype(F32) for x in smalls)
    edges = []
    for j in range(lanes // 128):
        edge = [grads[2 * j + n, 2 * HALF : 2 * HALF + 16, :].astype(F32) for n in range(2)]
        edges.append(jnp.where(low_lanes((16, 128)), edge[0], swap_halves(edge[1])))
    edge = jnp.concatenate(edges, axis=1)
    next0, next1 = edge[0:1], edge[1:2]

    def beyond(taps, x, edge):
        last, prior = x[rows - 1 : rows], x[rows - 2 : rows - 1]
        return short(taps, edge[0:1], last, prior), short(taps, edge[1:2], edge[0:1], last)

    def backward(taps, grad, grad0, grad1):
        one = with_bottom(pltpu.roll(grad, rows - 1, axis=0), [grad0])
        two = with_bottom(pltpu.roll(grad, rows - 2, axis=0), [grad0, grad1])
        return short(taps, grad, one, two)

    key_short, value_short = short(kt, kf, *delayed(kf, before[0:2])), short(vt, vf, *delayed(vf, before[2:4]))
    key_a, key_b = beyond(kt, kf, after[0:2])
    value_a, value_b = beyond(vt, vf, after[2:4])
    outs[0][...] = backward(kt, gz * value_short, next0 * value_a, next1 * value_b).astype(BF)
    outs[1][...] = backward(vt, gz * key_short, next0 * key_a, next1 * key_b).astype(BF)


def clip_body(c, ins, smalls, outs):
    outs[0][...] = turn_in(ins[0]) * smalls[0][0:1, 0:1]


def tree_step(x, axis, step):
    return x + lax.ppermute(x, axis, [(i, i ^ step) for i in range(lax.axis_size(axis))])


def shards(gate_in, key_in, value_in, conv_out, cotangent, long_filter, key_taps, value_taps, *, parts, others):
    rows, columns = key_in.shape
    shape = jax.ShapeDtypeStruct
    block = shape((rows, columns), BF)
    send_shape = shape((parts, 3 * HALF, rows), BF)
    tails = jnp.concatenate([key_in[-2:], value_in[-2:]], axis=0)
    heads = jnp.concatenate([key_in[:2], value_in[:2]], axis=0)
    before = lax.ppermute(tails, "seq", [(i, i + 1) for i in range(parts - 1)])
    (known,) = stream(
        known_body,
        "known",
        (cotangent, gate_in, long_filter),
        (),
        (send_shape,),
        ((0, (0, HALF)), (0, (2 * HALF, HALF))),
        4,
        60,
    )
    (send,) = stream(
        mixed_body,
        "mixed",
        (key_in, value_in),
        (key_taps, value_taps, before),
        (send_shape,),
        ((0, (HALF, HALF)),),
        4,
        60,
        alias=known,
    )
    recv = lax.all_to_all(send, "seq", 0, 0)
    send, heads = lax.optimization_barrier((send, heads))
    after = lax.ppermute(heads, "seq", [(i + 1, i) for i in range(parts - 1)])
    (gate_grad,) = stream(gate_body, "gate", (cotangent, conv_out), (), (block,), ((0, None),), 4, 16)
    recv, gate_grad, after = lax.optimization_barrier((recv, gate_grad, after))
    gz_send, gh_send = spectral(recv, parts, rows)
    gz_recv = lax.all_to_all(gz_send, "seq", 0, 0)
    gz_recv, gh_send = lax.optimization_barrier((gz_recv, gh_send))
    gh_recv = lax.all_to_all(gh_send, "seq", 0, 0)
    (taps,) = stream(
        taps_body,
        "taps",
        (gz_recv, key_in, value_in),
        (key_taps, value_taps, before),
        (shape((8, columns), F32),),
        ((0, None),),
        4,
        LATE_LIMIT,
    )
    late, taps = lax.optimization_barrier((gz_recv, taps))
    key_grad, value_grad = stream(
        inputs_body,
        "inputs",
        (late, key_in, value_in),
        (key_taps, value_taps, before, after),
        (block, block),
        ((0, None), (1, None)),
        4,
        LATE_LIMIT,
    )
    total = jnp.sum(late[:, 2 * HALF + 2 : 2 * HALF + 4, :].astype(F32), axis=(0, 1))
    total = jnp.broadcast_to(total[None], (8, total.shape[0]))
    step, other, turns = 1, 1, 0
    while 2 * step < parts:
        if turns % 2 == 1 and other < others:
            taps, total = lax.optimization_barrier((taps, total))
            total = tree_step(total, "chan", other)
            other *= 2
        taps = tree_step(taps, "seq", step)
        step *= 2
        turns += 1
        if turns == 2:
            taps, key_grad, value_grad = lax.optimization_barrier((taps, key_grad, value_grad))
    while other < others:
        total = tree_step(total, "chan", other)
        other *= 2
    count = rows * columns * parts * others
    scale = jnp.minimum(1.0, 1.0 / jnp.sqrt(total / count + 1e-6))
    taps, gh_recv = lax.optimization_barrier((taps, gh_recv))
    taps = tree_step(taps, "seq", parts // 2)
    (filter_grad,) = stream(
        clip_body, "clip", (gh_recv,), (scale,), (shape((rows, columns), F32),), ((0, None),), 4, LATE_LIMIT
    )
    return (gate_grad, key_grad, value_grad, filter_grad, taps[0:3], taps[3:6])


def solution(mesh):
    blocks, vectors = P("seq", "chan"), P(None, "chan")
    return jax.shard_map(
        functools.partial(shards, parts=mesh.shape["seq"], others=mesh.shape["chan"]),
        mesh=mesh,
        in_specs=(blocks,) * 6 + (vectors,) * 2,
        out_specs=(blocks,) * 4 + (vectors,) * 2,
        check_vma=False,
    )
```

```python
import functools
import math

import jax
import jax.numpy as jnp
import numpy as np
from jax import lax
from jax.experimental import pallas as pl
from jax.experimental.pallas import tpu as pltpu
from jax.sharding import PartitionSpec as P

BF = jnp.bfloat16
F32 = jnp.float32
HALF = 64
MIB = 1 << 20
SPECTRAL_LIMIT = 60
LATE_LIMIT = 24


def transform_tables(parts, rows):
    length = parts * rows
    mid = rows // 2
    p = np.arange(parts)
    k = np.arange(parts)
    step = math.pi / (2 * length)
    angle = ((rows * p[None, :] * (4 * k[:, None] + 1)) % (4 * length)) * step
    first = np.stack([np.cos(angle), -np.sin(angle)], 1)
    forward = np.einsum("kcp,rs->kcrps", first, np.eye(8)).reshape(parts * 16, parts * 8)
    backward = forward.T / length
    angle = ((np.arange(rows)[None, :] * (4 * k[:, None] + 1)) % (4 * length)) * step
    factors = np.stack([np.cos(angle), np.sin(angle)], 1).astype(np.float32)
    r, j = np.arange(mid)[:, None], np.arange(mid)[None, :]
    second = []
    for odd in (0, 1):
        turn = (((2 * j + odd) * r) % rows) * (2 * math.pi / rows)
        cos, sin = np.cos(turn), np.sin(turn)
        second.append(np.block([[cos, -sin], [sin, cos]]))
    as_bf = lambda x: x.astype(np.float32).astype(jnp.bfloat16)
    second = np.stack(second)
    return as_bf(forward), as_bf(second), as_bf(second.transpose(0, 2, 1)), as_bf(backward), factors


def low_lanes(shape):
    return (lax.broadcasted_iota(jnp.int32, shape, len(shape) - 1) % 128) < HALF


def swap_halves(x):
    return pltpu.roll(x, HALF, axis=x.ndim - 1)


def spectral_kernel(recv, m1, w, wi, m2, factors, gz_out, gh_out, x_v, gz_v, gh_v, y, u, in_sems, out_sems):
    parts, mid = recv.shape[0], recv.shape[2]
    rows = 2 * mid
    chans = (recv.shape[1] - 16) // 6
    group = parts
    pieces = 3

    def fetch(row, count, n):
        at = pl.ds(row, count)
        return pltpu.make_async_copy(recv.at[:, at, :], x_v.at[:, at, :], in_sems.at[n])

    def fetches(i):
        return [fetch(pl.multiple_of(3 * chans * h + chans * i, 16), chans, 2 * i + h) for h in range(2)]

    edges_in = fetch(6 * chans, 16, 2 * pieces)
    mixed_in, others_in = fetches(1), fetches(2) + fetches(0)
    for copy in [edges_in] + mixed_in + others_in:
        copy.start()

    for copy in [edges_in] + mixed_in:
        copy.wait()
    edges = x_v[:, 6 * chans : 6 * chans + 16, :].astype(F32)
    edges = edges[:, :8] + edges[:, 8:]
    ahead = jnp.concatenate([jnp.zeros((1, 8, 128), F32), edges[:-1]], axis=0)
    shorts = edges + pltpu.roll(ahead, 4, axis=1)
    starts = shorts * pltpu.roll(shorts, 6, axis=1)
    lane = lax.broadcasted_iota(jnp.int32, (chans, mid), 1)
    for p in range(parts):
        if p % 16 == 0:
            turned = starts[p : p + 16].reshape(128, 128).T[:chans]
        here = pltpu.roll(turned, (128 - 8 * (p % 16)) % 128, axis=1)
        old = x_v[p, chans : 2 * chans, :].astype(F32)
        x_v[p, chans : 2 * chans, :] = jnp.where(lane < 2, here, old).astype(BF)

    def forward(base):
        halves = [x_v[:, pl.ds(pl.multiple_of(3 * chans * h + base, 16), 16), :] for h in range(2)]
        x = jnp.concatenate(halves, axis=2).astype(F32)
        out = []
        for q in range(2):
            xq = x[:, 8 * q : 8 * q + 8, :].reshape(parts * 8, rows).astype(BF)
            out.append(jnp.dot(m1[...], xq, preferred_element_type=F32))
        for k in range(parts):
            c, s = factors[k, 0:1, :], factors[k, 1:2, :]
            sums, gaps = [], []
            for q in range(2):
                re, im = out[q][16 * k : 16 * k + 8], out[q][16 * k + 8 : 16 * k + 16]
                turned = (re * c + im * s, im * c - re * s)
                sums.append(jnp.concatenate([t[:, :mid] + t[:, mid:] for t in turned], axis=1))
                gaps.append(jnp.concatenate([t[:, :mid] - t[:, mid:] for t in turned], axis=1))
            y[0, k, pl.ds(base, 16), :] = jnp.concatenate(sums, axis=0).astype(BF)
            y[1, k, pl.ds(base, 16), :] = jnp.concatenate(gaps, axis=0).astype(BF)

    @pl.loop(1, pieces + 1)
    def _(n):
        i = lax.rem(n, pieces)

        @pl.when(i != 1)
        def _():
            for copy in fetches(i):
                copy.wait()

        for q in range(chans // 16):
            forward(pl.multiple_of(chans * i + 16 * q, 16))

    @pl.loop(0, parts // group)
    def _(kk):
        backs = []
        for odd in range(2):
            lines = y[odd, pl.ds(group * kk, group)].reshape(group * 3 * chans, rows)
            spec = jnp.dot(lines, w[odd], preferred_element_type=F32)
            products = []
            for n in range(group):
                at = 3 * chans * n
                grad = spec[at + 2 * chans : at + 3 * chans]
                gr, gi = grad[:, :mid], grad[:, mid:]
                for h in range(2):
                    part = spec[at + h * chans : at + (h + 1) * chans]
                    sr, si = part[:, :mid], part[:, mid:]
                    products.append(jnp.concatenate([sr * gr + si * gi, sr * gi - si * gr], axis=1))
            product = jnp.concatenate(products, axis=0).astype(BF)
            backs.append(jnp.dot(product, wi[odd], preferred_element_type=F32))
        for h, back in enumerate((backs[0] + backs[1], backs[0] - backs[1])):
            cols = slice(mid * h, mid * h + mid)
            for n in range(group):
                k = group * kk + n
                c, s = factors[k, 0:1, cols], factors[k, 1:2, cols]
                lines = back[2 * chans * n : 2 * chans * (n + 1)]
                re, im = lines[:, :mid], lines[:, mid:]
                u[2 * k, :, cols] = (re * c - im * s).astype(BF)
                u[2 * k + 1, :, cols] = (im * c + re * s).astype(BF)

    def backward(base):
        piece = u[:, pl.ds(base, 16), :].astype(F32)
        outs = []
        for q in range(2):
            v = piece[:, 8 * q : 8 * q + 8, :].reshape(parts * 16, rows).astype(BF)
            out = jnp.dot(m2[...], v, preferred_element_type=F32)
            outs.append(out.reshape(parts, 8, rows))
        return jnp.concatenate(outs, axis=1)

    tiles = chans // 16

    def store(target, scratch, first, row):
        at = pl.ds(row, 16)
        return pltpu.make_async_copy(scratch.at[:, at, :], target.at[:, at, :], out_sems.at[first])

    squares = jnp.zeros((8, rows), F32)
    for i in range(tiles):
        grad = backward(chans + 16 * i)
        for h in range(2):
            row = chans * h + 16 * i
            gh_v[:, row : row + 16, :] = grad[:, :, mid * h : mid * h + mid].astype(BF)
            store(gh_out, gh_v, tiles * h + i, row).start()
        squares += jnp.sum((grad * grad).reshape(parts * 2, 8, rows), axis=0)
    for i in range(tiles):
        grad = backward(16 * i)
        for h in range(2):
            row = chans * h + 16 * i
            gz_v[:, row : row + 16, :] = grad[:, :, mid * h : mid * h + mid].astype(BF)
            store(gz_out, gz_v, 2 * tiles + tiles * h + i, row).start()

    total = jnp.sum(jnp.sum(squares, axis=0, keepdims=True), axis=1, keepdims=True)
    coarse = total.astype(BF).astype(F32)
    fine = (total - coarse).astype(BF).astype(F32)
    row = lax.broadcasted_iota(jnp.int32, (16, 128), 0)
    sums = jnp.where(row == 2, coarse, jnp.where(row == 3, fine, 0.0))
    for p in range(parts):
        after = jnp.zeros((16, 128), F32)
        if p + 1 < parts:
            at = (p + 1) // 2 * 2
            after = gz_v[at : at + 2, :chans, :].reshape(2 * chans, mid).T[:16].astype(F32)
            if (p + 1) % 2:
                after = swap_halves(after)
        gz_v[p, 2 * chans : 2 * chans + 16, :] = jnp.where(row < 2, after, sums).astype(BF)
    store(gz_out, gz_v, 4 * tiles, 2 * chans).start()
    for n in range(2 * tiles):
        store(gh_out, gh_v, n, 16 * n).wait()
        store(gz_out, gz_v, 2 * tiles + n, 16 * n).wait()
    store(gz_out, gz_v, 4 * tiles, 2 * chans).wait()


def spectral(recv, parts, rows):
    tables = transform_tables(parts, rows)
    chans = (recv.shape[1] - 16) // 6
    mid = rows // 2
    vmem = pl.BlockSpec(memory_space=pltpu.VMEM)
    anywhere = pl.BlockSpec(memory_space=pl.ANY)
    flops = 2 * parts * parts * 16 * 8 * rows * chans // 8 * 5 + 2 * parts * rows * rows * chans * 10
    return pl.pallas_call(
        spectral_kernel,
        out_shape=(
            jax.ShapeDtypeStruct((parts, 2 * chans + 16, mid), BF),
            jax.ShapeDtypeStruct((parts, 2 * chans, mid), BF),
        ),
        in_specs=[anywhere] + [vmem] * 5,
        out_specs=(anywhere, anywhere),
        scratch_shapes=[
            pltpu.VMEM(recv.shape, BF),
            pltpu.VMEM((parts, 2 * chans + 16, mid), BF),
            pltpu.VMEM((parts, 2 * chans, mid), BF),
            pltpu.VMEM((2, parts, 3 * chans, rows), BF),
            pltpu.VMEM((2 * parts, 2 * chans, rows), BF),
            pltpu.SemaphoreType.DMA((7,)),
            pltpu.SemaphoreType.DMA((4 * (chans // 16) + 1,)),
        ],
        compiler_params=pltpu.CompilerParams(vmem_limit_bytes=SPECTRAL_LIMIT * MIB),
        cost_estimate=pl.CostEstimate(flops=flops, bytes_accessed=7 * MIB, transcendentals=0),
        name="spectral",
    )(recv, *[jnp.asarray(x) for x in tables])


def row_index(x):
    return lax.broadcasted_iota(jnp.int32, x.shape, 0)


def with_top(x, rows):
    top = x[:8]
    for n, line in enumerate(rows):
        top = jnp.where(row_index(top) == n, line, top)
    return jnp.concatenate([top, x[8:]], axis=0)


def with_bottom(x, rows):
    end = x.shape[0]
    bottom = x[end - 8 :]
    for n, line in enumerate(rows):
        bottom = jnp.where(row_index(bottom) == 8 - len(rows) + n, line, bottom)
    return jnp.concatenate([x[: end - 8], bottom], axis=0)


def delayed(x, before):
    first, second = before[0:1], before[1:2]
    one = with_top(pltpu.roll(x, 1, axis=0), [second])
    two = with_top(pltpu.roll(x, 2, axis=0), [first, second])
    return one, two


def stream(body, name, ins, smalls, outs, parts_of, chunks, limit):
    def size(shape):
        return (shape[0] // chunks,) + tuple(shape[1:]) if len(shape) == 3 else (shape[0], shape[1] // chunks)

    def window(ref, c, rows=None):
        if len(ref.shape) == 2:
            per = ref.shape[1] // chunks
            return ref.at[:, pl.ds(pl.multiple_of(c * per, 128), per)]
        per = ref.shape[0] // chunks
        at = ref.at[pl.ds(c * per, per)]
        return at if rows is None else ref.at[pl.ds(c * per, per), pl.ds(rows[0], rows[1]), :]

    n_in, n_small, n_out, n_part = len(ins), len(smalls), len(outs), len(parts_of)

    def kernel(*refs):
        refs = list(refs)
        take = lambda n: [refs.pop(0) for _ in range(n)]
        in_refs, small_refs, out_refs = take(n_in), take(n_small), take(n_out)
        in_v, small_v, out_v = take(n_in), take(n_small), take(n_part)
        in_sems, small_sems, out_sems = refs

        def fetch(n, c):
            return pltpu.make_async_copy(window(in_refs[n], c), in_v[n].at[c], in_sems.at[n, c])

        def store(n, c):
            index, rows = parts_of[n]
            return pltpu.make_async_copy(out_v[n].at[c], window(out_refs[index], c, rows), out_sems.at[n, c])

        smalls_in = [pltpu.make_async_copy(small_refs[n], small_v[n], small_sems.at[n]) for n in range(n_small)]
        for copy in smalls_in:
            copy.start()
        for c in range(chunks):
            for n in range(n_in):
                fetch(n, c).start()
        for copy in smalls_in:
            copy.wait()

        @pl.loop(0, chunks)
        def _(c):
            for n in range(n_in):
                fetch(n, c).wait()
            body(c, [v.at[c] for v in in_v], small_v, [v.at[c] for v in out_v])
            for n in range(n_part):
                store(n, c).start()

        for c in range(chunks):
            for n in range(n_part):
                store(n, c).wait()

    scratch = [pltpu.VMEM((chunks,) + size(a.shape), a.dtype) for a in ins]
    scratch += [pltpu.VMEM(a.shape, a.dtype) for a in smalls]
    for index, rows in parts_of:
        shape = size(outs[index].shape)
        if rows is not None:
            shape = (shape[0], rows[1], shape[2])
        scratch.append(pltpu.VMEM((chunks,) + shape, outs[index].dtype))
    scratch += [pltpu.SemaphoreType.DMA((n_in, chunks)), pltpu.SemaphoreType.DMA((max(n_small, 1),)), pltpu.SemaphoreType.DMA((n_part, chunks))]
    total = sum(math.prod(a.shape) * a.dtype.itemsize for a in list(ins) + list(outs))
    anywhere = pl.BlockSpec(memory_space=pl.ANY)
    return pl.pallas_call(
        kernel,
        in_specs=[anywhere] * (n_in + n_small),
        out_specs=[anywhere] * n_out,
        out_shape=outs,
        scratch_shapes=scratch,
        compiler_params=pltpu.CompilerParams(vmem_limit_bytes=limit * MIB),
        cost_estimate=pl.CostEstimate(flops=total, bytes_accessed=total, transcendentals=0),
        name=name,
    )(*ins, *smalls)


def columns_of(ref, c, lanes):
    return ref[:, pl.ds(pl.multiple_of(c * lanes, 128), lanes)]


def short(taps, x0, x1, x2):
    return taps[0:1] * x0 + taps[1:2] * x1 + taps[2:3] * x2


def pack_body(c, ins, smalls, outs):
    cot, gate, filt, key, value = ins
    out = outs[0]
    rows, lanes = cot.shape
    mid = rows // 2
    kt, vt = (columns_of(x, c, lanes) for x in smalls)
    none = jnp.zeros((2, lanes), F32)
    edges, shorts = [[], []], []
    for x, taps in ((key, kt), (value, vt)):
        x = x[...].astype(F32)
        shorts.append(short(taps, x, *delayed(x, none)))
        last, prior = x[rows - 1 : rows], x[rows - 2 : rows - 1]
        edges[0].append(shorts[-1][0:2])
        edges[1] += [taps[1:2] * last + taps[2:3] * prior, taps[2:3] * last]
    edge = jnp.concatenate(edges[0] + edges[1], axis=0)
    coarse = edge.astype(BF).astype(F32)
    edge = jnp.concatenate([coarse, edge - coarse], axis=0)
    grad = cot[...].astype(F32) * gate[...].astype(F32)
    for n, x in enumerate((filt[...], shorts[0] * shorts[1], grad)):
        x = x.astype(BF)
        for j in range(lanes // 128):
            for h in range(2):
                turned = x[mid * h : mid * h + mid, 128 * j : 128 * j + 128].T
                at = 3 * HALF * h + HALF * n
                out[2 * j, at : at + HALF] = turned[:HALF]
                out[2 * j + 1, at : at + HALF] = turned[HALF:]
    for j in range(lanes // 128):
        tile = edge[:, 128 * j : 128 * j + 128]
        out[2 * j, 6 * HALF :] = tile.astype(BF)
        out[2 * j + 1, 6 * HALF :] = swap_halves(tile).astype(BF)


def gate_body(c, ins, smalls, outs):
    cot, conv = ins
    outs[0][...] = (cot[...].astype(F32) * conv[...].astype(F32)).astype(BF)


def turn_in(blocks):
    tiles = []
    for j in range(blocks.shape[0] // 2):
        pair = (blocks[2 * j], blocks[2 * j + 1])
        halves = [jnp.concatenate([x[at : at + HALF] for x in pair], axis=0).T for at in (0, HALF)]
        tiles.append(jnp.concatenate(halves, axis=0))
    return jnp.concatenate(tiles, axis=1).astype(F32)


def taps_body(c, ins, smalls, outs):
    grads, key, value = ins
    gz = turn_in(grads)
    kf, vf = key[...].astype(F32), value[...].astype(F32)
    kt, vt, before = (columns_of(x, c, kf.shape[1]).astype(F32) for x in smalls)
    ks, vs = (kf,) + delayed(kf, before[0:2]), (vf,) + delayed(vf, before[2:4])
    grad_key, grad_value = gz * short(vt, *vs), gz * short(kt, *ks)
    sums = [jnp.sum(grad_key * x, axis=0, keepdims=True) for x in ks]
    sums += [jnp.sum(grad_value * x, axis=0, keepdims=True) for x in vs]
    outs[0][...] = jnp.concatenate(sums + [jnp.zeros((2, kf.shape[1]), F32)], axis=0)


def inputs_body(c, ins, smalls, outs):
    grads, key, value = ins
    rows, lanes = key.shape
    gz = turn_in(grads)
    kf, vf = key[...].astype(F32), value[...].astype(F32)
    kt, vt, before, after = (columns_of(x, c, lanes).astype(F32) for x in smalls)
    edges = []
    for j in range(lanes // 128):
        edge = [grads[2 * j + n, 2 * HALF : 2 * HALF + 16, :].astype(F32) for n in range(2)]
        edges.append(jnp.where(low_lanes((16, 128)), edge[0], swap_halves(edge[1])))
    edge = jnp.concatenate(edges, axis=1)
    next0, next1 = edge[0:1], edge[1:2]

    def beyond(taps, x, edge):
        last, prior = x[rows - 1 : rows], x[rows - 2 : rows - 1]
        return short(taps, edge[0:1], last, prior), short(taps, edge[1:2], edge[0:1], last)

    def backward(taps, grad, grad0, grad1):
        one = with_bottom(pltpu.roll(grad, rows - 1, axis=0), [grad0])
        two = with_bottom(pltpu.roll(grad, rows - 2, axis=0), [grad0, grad1])
        return short(taps, grad, one, two)

    key_short, value_short = short(kt, kf, *delayed(kf, before[0:2])), short(vt, vf, *delayed(vf, before[2:4]))
    key_a, key_b = beyond(kt, kf, after[0:2])
    value_a, value_b = beyond(vt, vf, after[2:4])
    outs[0][...] = backward(kt, gz * value_short, next0 * value_a, next1 * value_b).astype(BF)
    outs[1][...] = backward(vt, gz * key_short, next0 * key_a, next1 * key_b).astype(BF)


def clip_body(c, ins, smalls, outs):
    outs[0][...] = turn_in(ins[0]) * smalls[0][0:1, 0:1]


def tree_step(x, axis, step):
    return x + lax.ppermute(x, axis, [(i, i ^ step) for i in range(lax.axis_size(axis))])


def quarter_sum(x, axis):
    size = lax.axis_size(axis)
    one, two, three = (lax.ppermute(x, axis, [(i, (i + n * size // 4) % size) for i in range(size)]) for n in (1, 2, 3))
    return (x + two) + (one + three)


def shards(gate_in, key_in, value_in, conv_out, cotangent, long_filter, key_taps, value_taps, *, parts, others):
    rows, columns = key_in.shape
    shape = jax.ShapeDtypeStruct
    block = shape((rows, columns), BF)
    tails = jnp.concatenate([key_in[-2:], value_in[-2:]], axis=0)
    heads = jnp.concatenate([key_in[:2], value_in[:2]], axis=0)
    (send,) = stream(
        pack_body,
        "pack",
        (cotangent, gate_in, long_filter, key_in, value_in),
        (key_taps, value_taps),
        (shape((parts, 6 * HALF + 16, rows // 2), BF),),
        ((0, None),),
        4,
        60,
    )
    recv = lax.all_to_all(send, "seq", 0, 0)
    send, tails, heads = lax.optimization_barrier((send, tails, heads))
    before = lax.ppermute(tails, "seq", [(i, i + 1) for i in range(parts - 1)])
    after = lax.ppermute(heads, "seq", [(i + 1, i) for i in range(parts - 1)])
    (gate_grad,) = stream(gate_body, "gate", (cotangent, conv_out), (), (block,), ((0, None),), 4, 16)
    recv, gate_grad, before, after = lax.optimization_barrier((recv, gate_grad, before, after))
    gz_send, gh_send = spectral(recv, parts, rows)
    gz_recv = lax.all_to_all(gz_send, "seq", 0, 0)
    gz_recv, gh_send = lax.optimization_barrier((gz_recv, gh_send))
    gh_recv = lax.all_to_all(gh_send, "seq", 0, 0)
    (taps,) = stream(
        taps_body,
        "taps",
        (gz_recv, key_in, value_in),
        (key_taps, value_taps, before),
        (shape((8, columns), F32),),
        ((0, None),),
        4,
        LATE_LIMIT,
    )
    late, taps = lax.optimization_barrier((gz_recv, taps))
    total = jnp.sum(late[:, 2 * HALF + 2 : 2 * HALF + 4, :].astype(F32), axis=(0, 1))
    total = jnp.broadcast_to(total[None], (8, total.shape[0]))
    taps = tree_step(taps, "seq", 1)
    late, taps = lax.optimization_barrier((late, taps))
    key_grad, value_grad = stream(
        inputs_body,
        "inputs",
        (late, key_in, value_in),
        (key_taps, value_taps, before, after),
        (block, block),
        ((0, None), (1, None)),
        4,
        LATE_LIMIT,
    )
    taps = quarter_sum(taps, "seq")
    total = tree_step(total, "chan", 1)
    taps, total, key_grad, value_grad = lax.optimization_barrier((taps, total, key_grad, value_grad))
    total = tree_step(total, "chan", 3)
    taps = tree_step(taps, "seq", 2)
    count = rows * columns * parts * others
    scale = jnp.minimum(1.0, 1.0 / jnp.sqrt(total / count + 1e-6))
    taps, gh_recv = lax.optimization_barrier((taps, gh_recv))
    taps = tree_step(taps, "seq", 6)
    (filter_grad,) = stream(
        clip_body, "clip", (gh_recv,), (scale,), (shape((rows, columns), F32),), ((0, None),), 4, LATE_LIMIT
    )
    return (gate_grad, key_grad, value_grad, filter_grad, taps[0:3], taps[3:6])


def solution(mesh):
    blocks, vectors = P("seq", "chan"), P(None, "chan")
    return jax.shard_map(
        functools.partial(shards, parts=mesh.shape["seq"], others=mesh.shape["chan"]),
        mesh=mesh,
        in_specs=(blocks,) * 6 + (vectors,) * 2,
        out_specs=(blocks,) * 4 + (vectors,) * 2,
        check_vma=False,
    )
```

```python
import functools
import math

import jax
import jax.numpy as jnp
import numpy as np
from jax import lax
from jax.experimental import pallas as pl
from jax.experimental.pallas import tpu as pltpu
from jax.sharding import PartitionSpec as P

BF = jnp.bfloat16
F32 = jnp.float32
HALF = 64
MIB = 1 << 20
SPECTRAL_LIMIT = 60
LATE_LIMIT = 24


def transform_tables(parts, rows):
    length = parts * rows
    mid = rows // 2
    p = np.arange(parts)
    k = np.arange(parts)
    step = math.pi / (2 * length)
    angle = ((rows * p[None, :] * (4 * k[:, None] + 1)) % (4 * length)) * step
    first = np.stack([np.cos(angle), -np.sin(angle)], 1)
    forward = np.einsum("kcp,rs->kcrps", first, np.eye(8)).reshape(parts * 16, parts * 8)
    backward = forward.T / length
    angle = ((np.arange(rows)[None, :] * (4 * k[:, None] + 1)) % (4 * length)) * step
    factors = np.stack([np.cos(angle), np.sin(angle)], 1).astype(np.float32)
    r, j = np.arange(mid)[:, None], np.arange(mid)[None, :]
    second = []
    for odd in (0, 1):
        turn = (((2 * j + odd) * r) % rows) * (2 * math.pi / rows)
        cos, sin = np.cos(turn), np.sin(turn)
        second.append(np.block([[cos, -sin], [sin, cos]]))
    as_bf = lambda x: x.astype(np.float32).astype(jnp.bfloat16)
    second = np.stack(second)
    return as_bf(forward), as_bf(second), as_bf(second.transpose(0, 2, 1)), as_bf(backward), factors


def low_lanes(shape):
    return (lax.broadcasted_iota(jnp.int32, shape, len(shape) - 1) % 128) < HALF


def swap_halves(x):
    return pltpu.roll(x, HALF, axis=x.ndim - 1)


def spectral_kernel(recv, *refs):
    tables, (gz_out, gh_out), scratch = refs[:5], refs[5:7], refs[7:]
    m1, w, wi, m2, factors, x_v, gz_v, gh_v, y, u, in_sems, table_sems, out_sems = scratch
    parts, mid = recv.shape[0], recv.shape[2]
    rows = 2 * mid
    chans = (recv.shape[1] - 16) // 6
    group = parts
    pieces = 3

    def fetch(row, count, n):
        at = pl.ds(row, count)
        return pltpu.make_async_copy(recv.at[:, at, :], x_v.at[:, at, :], in_sems.at[n])

    def fetches(i):
        return [fetch(pl.multiple_of(3 * chans * h + chans * i, 16), chans, 2 * i + h) for h in range(2)]

    edges_in = fetch(6 * chans, 16, 2 * pieces)
    mixed_in, others_in = fetches(1), fetches(2) + fetches(0)
    tables_in = [pltpu.make_async_copy(tables[n], scratch[n], table_sems.at[n]) for n in range(5)]
    for copy in [edges_in] + mixed_in + [tables_in[0], tables_in[4]] + others_in + tables_in[1:4]:
        copy.start()

    for copy in [edges_in] + mixed_in:
        copy.wait()
    edges = x_v[:, 6 * chans : 6 * chans + 16, :].astype(F32)
    edges = edges[:, :8] + edges[:, 8:]
    ahead = jnp.concatenate([jnp.zeros((1, 8, 128), F32), edges[:-1]], axis=0)
    shorts = edges + pltpu.roll(ahead, 4, axis=1)
    starts = shorts * pltpu.roll(shorts, 6, axis=1)
    lane = lax.broadcasted_iota(jnp.int32, (chans, mid), 1)
    for p in range(parts):
        if p % 16 == 0:
            turned = starts[p : p + 16].reshape(128, 128).T[:chans]
        here = pltpu.roll(turned, (128 - 8 * (p % 16)) % 128, axis=1)
        old = x_v[p, chans : 2 * chans, :].astype(F32)
        x_v[p, chans : 2 * chans, :] = jnp.where(lane < 2, here, old).astype(BF)

    def forward(base):
        halves = [x_v[:, pl.ds(pl.multiple_of(3 * chans * h + base, 16), 16), :] for h in range(2)]
        x = jnp.concatenate(halves, axis=2).astype(F32)
        out = []
        for q in range(2):
            xq = x[:, 8 * q : 8 * q + 8, :].reshape(parts * 8, rows).astype(BF)
            out.append(jnp.dot(m1[...], xq, preferred_element_type=F32))
        for k in range(parts):
            c, s = factors[k, 0:1, :], factors[k, 1:2, :]
            sums, gaps = [], []
            for q in range(2):
                re, im = out[q][16 * k : 16 * k + 8], out[q][16 * k + 8 : 16 * k + 16]
                turned = (re * c + im * s, im * c - re * s)
                sums.append(jnp.concatenate([t[:, :mid] + t[:, mid:] for t in turned], axis=1))
                gaps.append(jnp.concatenate([t[:, :mid] - t[:, mid:] for t in turned], axis=1))
            y[0, k, pl.ds(base, 16), :] = jnp.concatenate(sums, axis=0).astype(BF)
            y[1, k, pl.ds(base, 16), :] = jnp.concatenate(gaps, axis=0).astype(BF)

    tables_in[0].wait()
    tables_in[4].wait()

    @pl.loop(1, pieces + 1)
    def _(n):
        i = lax.rem(n, pieces)

        @pl.when(i != 1)
        def _():
            for copy in fetches(i):
                copy.wait()

        for q in range(chans // 16):
            forward(pl.multiple_of(chans * i + 16 * q, 16))

    tables_in[1].wait()
    tables_in[2].wait()

    @pl.loop(0, parts // group)
    def _(kk):
        backs = []
        for odd in range(2):
            lines = y[odd, pl.ds(group * kk, group)].reshape(group * 3 * chans, rows)
            spec = jnp.dot(lines, w[odd], preferred_element_type=F32)
            products = []
            for n in range(group):
                at = 3 * chans * n
                grad = spec[at + 2 * chans : at + 3 * chans]
                gr, gi = grad[:, :mid], grad[:, mid:]
                for h in range(2):
                    part = spec[at + h * chans : at + (h + 1) * chans]
                    sr, si = part[:, :mid], part[:, mid:]
                    products.append(jnp.concatenate([sr * gr + si * gi, sr * gi - si * gr], axis=1))
            product = jnp.concatenate(products, axis=0).astype(BF)
            backs.append(jnp.dot(product, wi[odd], preferred_element_type=F32))
        for h, back in enumerate((backs[0] + backs[1], backs[0] - backs[1])):
            cols = slice(mid * h, mid * h + mid)
            for n in range(group):
                k = group * kk + n
                c, s = factors[k, 0:1, cols], factors[k, 1:2, cols]
                lines = back[2 * chans * n : 2 * chans * (n + 1)]
                re, im = lines[:, :mid], lines[:, mid:]
                u[2 * k, :, cols] = (re * c - im * s).astype(BF)
                u[2 * k + 1, :, cols] = (im * c + re * s).astype(BF)

    def backward(base):
        piece = u[:, pl.ds(base, 16), :].astype(F32)
        outs = []
        for q in range(2):
            v = piece[:, 8 * q : 8 * q + 8, :].reshape(parts * 16, rows).astype(BF)
            out = jnp.dot(m2[...], v, preferred_element_type=F32)
            outs.append(out.reshape(parts, 8, rows))
        return jnp.concatenate(outs, axis=1)

    tiles = chans // 16

    def store(target, scratch, first, row):
        at = pl.ds(row, 16)
        return pltpu.make_async_copy(scratch.at[:, at, :], target.at[:, at, :], out_sems.at[first])

    tables_in[3].wait()
    squares = jnp.zeros((8, rows), F32)
    for i in range(tiles):
        grad = backward(chans + 16 * i)
        for h in range(2):
            row = chans * h + 16 * i
            gh_v[:, row : row + 16, :] = grad[:, :, mid * h : mid * h + mid].astype(BF)
            store(gh_out, gh_v, tiles * h + i, row).start()
        squares += jnp.sum((grad * grad).reshape(parts * 2, 8, rows), axis=0)
    for i in range(tiles):
        grad = backward(16 * i)
        for h in range(2):
            row = chans * h + 16 * i
            gz_v[:, row : row + 16, :] = grad[:, :, mid * h : mid * h + mid].astype(BF)
            store(gz_out, gz_v, 2 * tiles + tiles * h + i, row).start()

    total = jnp.sum(jnp.sum(squares, axis=0, keepdims=True), axis=1, keepdims=True)
    coarse = total.astype(BF).astype(F32)
    fine = (total - coarse).astype(BF).astype(F32)
    row = lax.broadcasted_iota(jnp.int32, (16, 128), 0)
    sums = jnp.where(row == 2, coarse, jnp.where(row == 3, fine, 0.0))
    for p in range(parts):
        after = jnp.zeros((16, 128), F32)
        if p + 1 < parts:
            at = (p + 1) // 2 * 2
            after = gz_v[at : at + 2, :chans, :].reshape(2 * chans, mid).T[:16].astype(F32)
            if (p + 1) % 2:
                after = swap_halves(after)
        gz_v[p, 2 * chans : 2 * chans + 16, :] = jnp.where(row < 2, after, sums).astype(BF)
    store(gz_out, gz_v, 4 * tiles, 2 * chans).start()
    for n in range(2 * tiles):
        store(gh_out, gh_v, n, 16 * n).wait()
        store(gz_out, gz_v, 2 * tiles + n, 16 * n).wait()
    store(gz_out, gz_v, 4 * tiles, 2 * chans).wait()


def spectral(recv, parts, rows):
    tables = transform_tables(parts, rows)
    chans = (recv.shape[1] - 16) // 6
    mid = rows // 2
    anywhere = pl.BlockSpec(memory_space=pl.ANY)
    flops = 2 * parts * parts * 16 * 8 * rows * chans // 8 * 5 + 2 * parts * rows * rows * chans * 10
    return pl.pallas_call(
        spectral_kernel,
        out_shape=(
            jax.ShapeDtypeStruct((parts, 2 * chans + 16, mid), BF),
            jax.ShapeDtypeStruct((parts, 2 * chans, mid), BF),
        ),
        in_specs=[anywhere] * 6,
        out_specs=(anywhere, anywhere),
        scratch_shapes=[pltpu.VMEM(x.shape, x.dtype) for x in tables]
        + [
            pltpu.VMEM(recv.shape, BF),
            pltpu.VMEM((parts, 2 * chans + 16, mid), BF),
            pltpu.VMEM((parts, 2 * chans, mid), BF),
            pltpu.VMEM((2, parts, 3 * chans, rows), BF),
            pltpu.VMEM((2 * parts, 2 * chans, rows), BF),
            pltpu.SemaphoreType.DMA((7,)),
            pltpu.SemaphoreType.DMA((len(tables),)),
            pltpu.SemaphoreType.DMA((4 * (chans // 16) + 1,)),
        ],
        compiler_params=pltpu.CompilerParams(vmem_limit_bytes=SPECTRAL_LIMIT * MIB),
        cost_estimate=pl.CostEstimate(flops=flops, bytes_accessed=7 * MIB, transcendentals=0),
        name="spectral",
    )(recv, *[jnp.asarray(x) for x in tables])


def row_index(x):
    return lax.broadcasted_iota(jnp.int32, x.shape, 0)


def with_top(x, rows):
    top = x[:8]
    for n, line in enumerate(rows):
        top = jnp.where(row_index(top) == n, line, top)
    return jnp.concatenate([top, x[8:]], axis=0)


def with_bottom(x, rows):
    end = x.shape[0]
    bottom = x[end - 8 :]
    for n, line in enumerate(rows):
        bottom = jnp.where(row_index(bottom) == 8 - len(rows) + n, line, bottom)
    return jnp.concatenate([x[: end - 8], bottom], axis=0)


def delayed(x, before):
    first, second = before[0:1], before[1:2]
    one = with_top(pltpu.roll(x, 1, axis=0), [second])
    two = with_top(pltpu.roll(x, 2, axis=0), [first, second])
    return one, two


def stream(body, name, ins, smalls, outs, parts_of, chunks, limit):
    def size(shape):
        return (shape[0] // chunks,) + tuple(shape[1:]) if len(shape) == 3 else (shape[0], shape[1] // chunks)

    def window(ref, c, rows=None):
        if len(ref.shape) == 2:
            per = ref.shape[1] // chunks
            return ref.at[:, pl.ds(pl.multiple_of(c * per, 128), per)]
        per = ref.shape[0] // chunks
        at = ref.at[pl.ds(c * per, per)]
        return at if rows is None else ref.at[pl.ds(c * per, per), pl.ds(rows[0], rows[1]), :]

    n_in, n_small, n_out, n_part = len(ins), len(smalls), len(outs), len(parts_of)

    def kernel(*refs):
        refs = list(refs)
        take = lambda n: [refs.pop(0) for _ in range(n)]
        in_refs, small_refs, out_refs = take(n_in), take(n_small), take(n_out)
        in_v, small_v, out_v = take(n_in), take(n_small), take(n_part)
        in_sems, small_sems, out_sems = refs

        def fetch(n, c):
            return pltpu.make_async_copy(window(in_refs[n], c), in_v[n].at[c], in_sems.at[n, c])

        def store(n, c):
            index, rows = parts_of[n]
            return pltpu.make_async_copy(out_v[n].at[c], window(out_refs[index], c, rows), out_sems.at[n, c])

        smalls_in = [pltpu.make_async_copy(small_refs[n], small_v[n], small_sems.at[n]) for n in range(n_small)]
        for copy in smalls_in:
            copy.start()
        for c in range(chunks):
            for n in range(n_in):
                fetch(n, c).start(priority=(n + c) % 2)
        for copy in smalls_in:
            copy.wait()

        @pl.loop(0, chunks)
        def _(c):
            for n in range(n_in):
                fetch(n, c).wait()
            body(c, [v.at[c] for v in in_v], small_v, [v.at[c] for v in out_v])
            for n in range(n_part):
                store(n, c).start()

        for c in range(chunks):
            for n in range(n_part):
                store(n, c).wait()

    scratch = [pltpu.VMEM((chunks,) + size(a.shape), a.dtype) for a in ins]
    scratch += [pltpu.VMEM(a.shape, a.dtype) for a in smalls]
    for index, rows in parts_of:
        shape = size(outs[index].shape)
        if rows is not None:
            shape = (shape[0], rows[1], shape[2])
        scratch.append(pltpu.VMEM((chunks,) + shape, outs[index].dtype))
    scratch += [pltpu.SemaphoreType.DMA((n_in, chunks)), pltpu.SemaphoreType.DMA((max(n_small, 1),)), pltpu.SemaphoreType.DMA((n_part, chunks))]
    total = sum(math.prod(a.shape) * a.dtype.itemsize for a in list(ins) + list(outs))
    anywhere = pl.BlockSpec(memory_space=pl.ANY)
    return pl.pallas_call(
        kernel,
        in_specs=[anywhere] * (n_in + n_small),
        out_specs=[anywhere] * n_out,
        out_shape=outs,
        scratch_shapes=scratch,
        compiler_params=pltpu.CompilerParams(vmem_limit_bytes=limit * MIB),
        cost_estimate=pl.CostEstimate(flops=total, bytes_accessed=total, transcendentals=0),
        name=name,
    )(*ins, *smalls)


def columns_of(ref, c, lanes):
    return ref[:, pl.ds(pl.multiple_of(c * lanes, 128), lanes)]


def short(taps, x0, x1, x2):
    return taps[0:1] * x0 + taps[1:2] * x1 + taps[2:3] * x2


def pack_body(c, ins, smalls, outs):
    cot, gate, filt, key, value = ins
    out = outs[0]
    rows, lanes = cot.shape
    mid = rows // 2
    kt, vt = (columns_of(x, c, lanes) for x in smalls)
    none = jnp.zeros((2, lanes), F32)
    edges, shorts = [[], []], []
    for x, taps in ((key, kt), (value, vt)):
        x = x[...].astype(F32)
        shorts.append(short(taps, x, *delayed(x, none)))
        last, prior = x[rows - 1 : rows], x[rows - 2 : rows - 1]
        edges[0].append(shorts[-1][0:2])
        edges[1] += [taps[1:2] * last + taps[2:3] * prior, taps[2:3] * last]
    edge = jnp.concatenate(edges[0] + edges[1], axis=0)
    coarse = edge.astype(BF).astype(F32)
    edge = jnp.concatenate([coarse, edge - coarse], axis=0)
    grad = cot[...].astype(F32) * gate[...].astype(F32)
    for n, x in enumerate((filt[...], shorts[0] * shorts[1], grad)):
        x = x.astype(BF)
        for j in range(lanes // 128):
            for h in range(2):
                turned = x[mid * h : mid * h + mid, 128 * j : 128 * j + 128].T
                at = 3 * HALF * h + HALF * n
                out[2 * j, at : at + HALF] = turned[:HALF]
                out[2 * j + 1, at : at + HALF] = turned[HALF:]
    for j in range(lanes // 128):
        tile = edge[:, 128 * j : 128 * j + 128]
        out[2 * j, 6 * HALF :] = tile.astype(BF)
        out[2 * j + 1, 6 * HALF :] = swap_halves(tile).astype(BF)


def gate_body(c, ins, smalls, outs):
    cot, conv = ins
    outs[0][...] = (cot[...].astype(F32) * conv[...].astype(F32)).astype(BF)


def turn_in(blocks):
    tiles = []
    for j in range(blocks.shape[0] // 2):
        pair = (blocks[2 * j], blocks[2 * j + 1])
        halves = [jnp.concatenate([x[at : at + HALF] for x in pair], axis=0).T for at in (0, HALF)]
        tiles.append(jnp.concatenate(halves, axis=0))
    return jnp.concatenate(tiles, axis=1).astype(F32)


def taps_body(c, ins, smalls, outs):
    grads, key, value = ins
    gz = turn_in(grads)
    kf, vf = key[...].astype(F32), value[...].astype(F32)
    kt, vt, before = (columns_of(x, c, kf.shape[1]).astype(F32) for x in smalls)
    ks, vs = (kf,) + delayed(kf, before[0:2]), (vf,) + delayed(vf, before[2:4])
    grad_key, grad_value = gz * short(vt, *vs), gz * short(kt, *ks)
    sums = [jnp.sum(grad_key * x, axis=0, keepdims=True) for x in ks]
    sums += [jnp.sum(grad_value * x, axis=0, keepdims=True) for x in vs]
    outs[0][...] = jnp.concatenate(sums + [jnp.zeros((2, kf.shape[1]), F32)], axis=0)


def inputs_body(c, ins, smalls, outs):
    grads, key, value = ins
    rows, lanes = key.shape
    gz = turn_in(grads)
    kf, vf = key[...].astype(F32), value[...].astype(F32)
    kt, vt, before, after = (columns_of(x, c, lanes).astype(F32) for x in smalls)
    edges = []
    for j in range(lanes // 128):
        edge = [grads[2 * j + n, 2 * HALF : 2 * HALF + 16, :].astype(F32) for n in range(2)]
        edges.append(jnp.where(low_lanes((16, 128)), edge[0], swap_halves(edge[1])))
    edge = jnp.concatenate(edges, axis=1)
    next0, next1 = edge[0:1], edge[1:2]

    def beyond(taps, x, edge):
        last, prior = x[rows - 1 : rows], x[rows - 2 : rows - 1]
        return short(taps, edge[0:1], last, prior), short(taps, edge[1:2], edge[0:1], last)

    def backward(taps, grad, grad0, grad1):
        one = with_bottom(pltpu.roll(grad, rows - 1, axis=0), [grad0])
        two = with_bottom(pltpu.roll(grad, rows - 2, axis=0), [grad0, grad1])
        return short(taps, grad, one, two)

    key_short, value_short = short(kt, kf, *delayed(kf, before[0:2])), short(vt, vf, *delayed(vf, before[2:4]))
    key_a, key_b = beyond(kt, kf, after[0:2])
    value_a, value_b = beyond(vt, vf, after[2:4])
    outs[0][...] = backward(kt, gz * value_short, next0 * value_a, next1 * value_b).astype(BF)
    outs[1][...] = backward(vt, gz * key_short, next0 * key_a, next1 * key_b).astype(BF)


def clip_body(c, ins, smalls, outs):
    outs[0][...] = turn_in(ins[0]) * smalls[0][0:1, 0:1]


def tree_step(x, axis, step):
    return x + lax.ppermute(x, axis, [(i, i ^ step) for i in range(lax.axis_size(axis))])


def quarter_sum(x, axis):
    size = lax.axis_size(axis)
    one, two, three = (lax.ppermute(x, axis, [(i, (i + n * size // 4) % size) for i in range(size)]) for n in (1, 2, 3))
    return (x + two) + (one + three)


def shards(gate_in, key_in, value_in, conv_out, cotangent, long_filter, key_taps, value_taps, *, parts, others):
    rows, columns = key_in.shape
    shape = jax.ShapeDtypeStruct
    block = shape((rows, columns), BF)
    tails = jnp.concatenate([key_in[-2:], value_in[-2:]], axis=0)
    heads = jnp.concatenate([key_in[:2], value_in[:2]], axis=0)
    (send,) = stream(
        pack_body,
        "pack",
        (cotangent, gate_in, long_filter, key_in, value_in),
        (key_taps, value_taps),
        (shape((parts, 6 * HALF + 16, rows // 2), BF),),
        ((0, None),),
        4,
        60,
    )
    recv = lax.all_to_all(send, "seq", 0, 0)
    send, tails, heads = lax.optimization_barrier((send, tails, heads))
    before = lax.ppermute(tails, "seq", [(i, i + 1) for i in range(parts - 1)])
    after = lax.ppermute(heads, "seq", [(i + 1, i) for i in range(parts - 1)])
    (gate_grad,) = stream(gate_body, "gate", (cotangent, conv_out), (), (block,), ((0, None),), 4, 16)
    recv, gate_grad, before, after = lax.optimization_barrier((recv, gate_grad, before, after))
    gz_send, gh_send = spectral(recv, parts, rows)
    gz_recv = lax.all_to_all(gz_send, "seq", 0, 0)
    gz_recv, gh_send = lax.optimization_barrier((gz_recv, gh_send))
    gh_recv = lax.all_to_all(gh_send, "seq", 0, 0)
    (taps,) = stream(
        taps_body,
        "taps",
        (gz_recv, key_in, value_in),
        (key_taps, value_taps, before),
        (shape((8, columns), F32),),
        ((0, None),),
        4,
        LATE_LIMIT,
    )
    late, taps = lax.optimization_barrier((gz_recv, taps))
    total = jnp.sum(late[:, 2 * HALF + 2 : 2 * HALF + 4, :].astype(F32), axis=(0, 1))
    total = jnp.broadcast_to(total[None], (8, total.shape[0]))
    taps = tree_step(taps, "seq", 1)
    late, taps = lax.optimization_barrier((late, taps))
    key_grad, value_grad = stream(
        inputs_body,
        "inputs",
        (late, key_in, value_in),
        (key_taps, value_taps, before, after),
        (block, block),
        ((0, None), (1, None)),
        4,
        LATE_LIMIT,
    )
    taps = quarter_sum(taps, "seq")
    total = tree_step(total, "chan", 1)
    taps, total, key_grad, value_grad = lax.optimization_barrier((taps, total, key_grad, value_grad))
    total = tree_step(total, "chan", 3)
    taps = tree_step(taps, "seq", 2)
    count = rows * columns * parts * others
    scale = jnp.minimum(1.0, 1.0 / jnp.sqrt(total / count + 1e-6))
    taps, gh_recv = lax.optimization_barrier((taps, gh_recv))
    taps = tree_step(taps, "seq", 6)
    (filter_grad,) = stream(
        clip_body, "clip", (gh_recv,), (scale,), (shape((rows, columns), F32),), ((0, None),), 4, LATE_LIMIT
    )
    return (gate_grad, key_grad, value_grad, filter_grad, taps[0:3], taps[3:6])


def solution(mesh):
    blocks, vectors = P("seq", "chan"), P(None, "chan")
    return jax.shard_map(
        functools.partial(shards, parts=mesh.shape["seq"], others=mesh.shape["chan"]),
        mesh=mesh,
        in_specs=(blocks,) * 6 + (vectors,) * 2,
        out_specs=(blocks,) * 4 + (vectors,) * 2,
        check_vma=False,
    )
```

```python
import functools
import math

import jax
import jax.numpy as jnp
import numpy as np
from jax import lax
from jax.experimental import pallas as pl
from jax.experimental.pallas import tpu as pltpu
from jax.sharding import PartitionSpec as P

BF = jnp.bfloat16
F32 = jnp.float32
HALF = 64
MIB = 1 << 20
SPECTRAL_LIMIT = 60
LATE_LIMIT = 24


def transform_tables(parts, rows):
    length = parts * rows
    mid = rows // 2
    p = np.arange(parts)
    k = np.arange(parts)
    step = math.pi / (2 * length)
    angle = ((rows * p[None, :] * (4 * k[:, None] + 1)) % (4 * length)) * step
    first = np.stack([np.cos(angle), -np.sin(angle)], 1)
    forward = np.einsum("kcp,rs->kcrps", first, np.eye(8)).reshape(parts * 16, parts * 8)
    backward = forward.T / length
    angle = ((np.arange(rows)[None, :] * (4 * k[:, None] + 1)) % (4 * length)) * step
    factors = np.stack([np.cos(angle), np.sin(angle)], 1).astype(np.float32)
    r, j = np.arange(mid)[:, None], np.arange(mid)[None, :]
    second = []
    for odd in (0, 1):
        turn = (((2 * j + odd) * r) % rows) * (2 * math.pi / rows)
        cos, sin = np.cos(turn), np.sin(turn)
        second.append(np.block([[cos, -sin], [sin, cos]]))
    as_bf = lambda x: x.astype(np.float32).astype(jnp.bfloat16)
    second = np.stack(second)
    return as_bf(forward), as_bf(second), as_bf(second.transpose(0, 2, 1)), as_bf(backward), factors


def low_lanes(shape):
    return (lax.broadcasted_iota(jnp.int32, shape, len(shape) - 1) % 128) < HALF


def swap_halves(x):
    return pltpu.roll(x, HALF, axis=x.ndim - 1)


def spectral_kernel(recv, *refs):
    tables, (gz_out, gh_out), scratch = refs[:5], refs[5:7], refs[7:]
    m1, w, wi, m2, factors, x_v, gz_v, gh_v, y, u, in_sems, table_sems, out_sems = scratch
    parts, mid = recv.shape[0], recv.shape[2]
    rows = 2 * mid
    chans = (recv.shape[1] - 16) // 6
    group = parts
    pieces = 3

    def fetch(row, count, n):
        at = pl.ds(row, count)
        return pltpu.make_async_copy(recv.at[:, at, :], x_v.at[:, at, :], in_sems.at[n])

    def fetches(i):
        return [fetch(pl.multiple_of(3 * chans * h + chans * i, 16), chans, 2 * i + h) for h in range(2)]

    edges_in = fetch(6 * chans, 16, 2 * pieces)
    mixed_in, others_in = fetches(1), fetches(2) + fetches(0)
    tables_in = [pltpu.make_async_copy(tables[n], scratch[n], table_sems.at[n]) for n in range(5)]
    for copy in [edges_in] + mixed_in + [tables_in[0], tables_in[4]] + others_in + tables_in[1:4]:
        copy.start()

    for copy in [edges_in] + mixed_in:
        copy.wait()
    edges = x_v[:, 6 * chans : 6 * chans + 16, :].astype(F32)
    edges = edges[:, :8] + edges[:, 8:]
    ahead = jnp.concatenate([jnp.zeros((1, 8, 128), F32), edges[:-1]], axis=0)
    shorts = edges + pltpu.roll(ahead, 4, axis=1)
    starts = shorts * pltpu.roll(shorts, 6, axis=1)
    lane = lax.broadcasted_iota(jnp.int32, (chans, mid), 1)
    for p in range(parts):
        if p % 16 == 0:
            turned = starts[p : p + 16].reshape(128, 128).T[:chans]
        here = pltpu.roll(turned, (128 - 8 * (p % 16)) % 128, axis=1)
        old = x_v[p, chans : 2 * chans, :].astype(F32)
        x_v[p, chans : 2 * chans, :] = jnp.where(lane < 2, here, old).astype(BF)

    def forward(base):
        halves = [x_v[:, pl.ds(pl.multiple_of(3 * chans * h + base, 16), 16), :] for h in range(2)]
        x = jnp.concatenate(halves, axis=2).astype(F32)
        out = []
        for q in range(2):
            xq = x[:, 8 * q : 8 * q + 8, :].reshape(parts * 8, rows).astype(BF)
            out.append(jnp.dot(m1[...], xq, preferred_element_type=F32))
        for k in range(parts):
            c, s = factors[k, 0:1, :], factors[k, 1:2, :]
            sums, gaps = [], []
            for q in range(2):
                re, im = out[q][16 * k : 16 * k + 8], out[q][16 * k + 8 : 16 * k + 16]
                turned = (re * c + im * s, im * c - re * s)
                sums.append(jnp.concatenate([t[:, :mid] + t[:, mid:] for t in turned], axis=1))
                gaps.append(jnp.concatenate([t[:, :mid] - t[:, mid:] for t in turned], axis=1))
            y[0, k, pl.ds(base, 16), :] = jnp.concatenate(sums, axis=0).astype(BF)
            y[1, k, pl.ds(base, 16), :] = jnp.concatenate(gaps, axis=0).astype(BF)

    tables_in[0].wait()
    tables_in[4].wait()

    @pl.loop(1, pieces + 1)
    def _(n):
        i = lax.rem(n, pieces)

        @pl.when(i != 1)
        def _():
            for copy in fetches(i):
                copy.wait()

        for q in range(chans // 16):
            forward(pl.multiple_of(chans * i + 16 * q, 16))

    tables_in[1].wait()
    tables_in[2].wait()

    @pl.loop(0, parts // group)
    def _(kk):
        backs = []
        for odd in range(2):
            lines = y[odd, pl.ds(group * kk, group)].reshape(group * 3 * chans, rows)
            spec = jnp.dot(lines, w[odd], preferred_element_type=F32)
            products = []
            for n in range(group):
                at = 3 * chans * n
                grad = spec[at + 2 * chans : at + 3 * chans]
                gr, gi = grad[:, :mid], grad[:, mid:]
                for h in range(2):
                    part = spec[at + h * chans : at + (h + 1) * chans]
                    sr, si = part[:, :mid], part[:, mid:]
                    products.append(jnp.concatenate([sr * gr + si * gi, sr * gi - si * gr], axis=1))
            product = jnp.concatenate(products, axis=0).astype(BF)
            backs.append(jnp.dot(product, wi[odd], preferred_element_type=F32))
        for h, back in enumerate((backs[0] + backs[1], backs[0] - backs[1])):
            cols = slice(mid * h, mid * h + mid)
            for n in range(group):
                k = group * kk + n
                c, s = factors[k, 0:1, cols], factors[k, 1:2, cols]
                lines = back[2 * chans * n : 2 * chans * (n + 1)]
                re, im = lines[:, :mid], lines[:, mid:]
                u[2 * k, :, cols] = (re * c - im * s).astype(BF)
                u[2 * k + 1, :, cols] = (im * c + re * s).astype(BF)

    def backward(base):
        piece = u[:, pl.ds(base, 16), :].astype(F32)
        outs = []
        for q in range(2):
            v = piece[:, 8 * q : 8 * q + 8, :].reshape(parts * 16, rows).astype(BF)
            out = jnp.dot(m2[...], v, preferred_element_type=F32)
            outs.append(out.reshape(parts, 8, rows))
        return jnp.concatenate(outs, axis=1)

    tiles = chans // 16

    def store(target, scratch, first, row):
        at = pl.ds(row, 16)
        return pltpu.make_async_copy(scratch.at[:, at, :], target.at[:, at, :], out_sems.at[first])

    tables_in[3].wait()
    squares = jnp.zeros((8, rows), F32)
    for i in range(tiles):
        grad = backward(chans + 16 * i)
        for h in range(2):
            row = chans * h + 16 * i
            gh_v[:, row : row + 16, :] = grad[:, :, mid * h : mid * h + mid].astype(BF)
            store(gh_out, gh_v, tiles * h + i, row).start()
        squares += jnp.sum((grad * grad).reshape(parts * 2, 8, rows), axis=0)
    for i in range(tiles):
        grad = backward(16 * i)
        for h in range(2):
            row = chans * h + 16 * i
            gz_v[:, row : row + 16, :] = grad[:, :, mid * h : mid * h + mid].astype(BF)
            store(gz_out, gz_v, 2 * tiles + tiles * h + i, row).start()

    total = jnp.sum(jnp.sum(squares, axis=0, keepdims=True), axis=1, keepdims=True)
    coarse = total.astype(BF).astype(F32)
    fine = (total - coarse).astype(BF).astype(F32)
    row = lax.broadcasted_iota(jnp.int32, (16, 128), 0)
    sums = jnp.where(row == 2, coarse, jnp.where(row == 3, fine, 0.0))
    for p in range(parts):
        after = jnp.zeros((16, 128), F32)
        if p + 1 < parts:
            at = (p + 1) // 2 * 2
            after = gz_v[at : at + 2, :chans, :].reshape(2 * chans, mid).T[:16].astype(F32)
            if (p + 1) % 2:
                after = swap_halves(after)
        gz_v[p, 2 * chans : 2 * chans + 16, :] = jnp.where(row < 2, after, sums).astype(BF)
    store(gz_out, gz_v, 4 * tiles, 2 * chans).start()
    for n in range(2 * tiles):
        store(gh_out, gh_v, n, 16 * n).wait()
        store(gz_out, gz_v, 2 * tiles + n, 16 * n).wait()
    store(gz_out, gz_v, 4 * tiles, 2 * chans).wait()


def spectral(recv, parts, rows):
    tables = transform_tables(parts, rows)
    chans = (recv.shape[1] - 16) // 6
    mid = rows // 2
    anywhere = pl.BlockSpec(memory_space=pl.ANY)
    flops = 2 * parts * parts * 16 * 8 * rows * chans // 8 * 5 + 2 * parts * rows * rows * chans * 10
    return pl.pallas_call(
        spectral_kernel,
        out_shape=(
            jax.ShapeDtypeStruct((parts, 2 * chans + 16, mid), BF),
            jax.ShapeDtypeStruct((parts, 2 * chans, mid), BF),
        ),
        in_specs=[anywhere] * 6,
        out_specs=(anywhere, anywhere),
        scratch_shapes=[pltpu.VMEM(x.shape, x.dtype) for x in tables]
        + [
            pltpu.VMEM(recv.shape, BF),
            pltpu.VMEM((parts, 2 * chans + 16, mid), BF),
            pltpu.VMEM((parts, 2 * chans, mid), BF),
            pltpu.VMEM((2, parts, 3 * chans, rows), BF),
            pltpu.VMEM((2 * parts, 2 * chans, rows), BF),
            pltpu.SemaphoreType.DMA((7,)),
            pltpu.SemaphoreType.DMA((len(tables),)),
            pltpu.SemaphoreType.DMA((4 * (chans // 16) + 1,)),
        ],
        compiler_params=pltpu.CompilerParams(vmem_limit_bytes=SPECTRAL_LIMIT * MIB),
        cost_estimate=pl.CostEstimate(flops=flops, bytes_accessed=7 * MIB, transcendentals=0),
        name="spectral",
    )(recv, *[jnp.asarray(x) for x in tables])


def row_index(x):
    return lax.broadcasted_iota(jnp.int32, x.shape, 0)


def with_top(x, rows):
    top = x[:8]
    for n, line in enumerate(rows):
        top = jnp.where(row_index(top) == n, line, top)
    return jnp.concatenate([top, x[8:]], axis=0)


def with_bottom(x, rows):
    end = x.shape[0]
    bottom = x[end - 8 :]
    for n, line in enumerate(rows):
        bottom = jnp.where(row_index(bottom) == 8 - len(rows) + n, line, bottom)
    return jnp.concatenate([x[: end - 8], bottom], axis=0)


def delayed(x, before):
    first, second = before[0:1], before[1:2]
    one = with_top(pltpu.roll(x, 1, axis=0), [second])
    two = with_top(pltpu.roll(x, 2, axis=0), [first, second])
    return one, two


def stream(body, name, ins, smalls, outs, parts_of, chunks, limit):
    def size(shape):
        return (shape[0] // chunks,) + tuple(shape[1:]) if len(shape) == 3 else (shape[0], shape[1] // chunks)

    def window(ref, c, rows=None):
        if len(ref.shape) == 2:
            per = ref.shape[1] // chunks
            return ref.at[:, pl.ds(pl.multiple_of(c * per, 128), per)]
        per = ref.shape[0] // chunks
        at = ref.at[pl.ds(c * per, per)]
        return at if rows is None else ref.at[pl.ds(c * per, per), pl.ds(rows[0], rows[1]), :]

    n_in, n_small, n_out, n_part = len(ins), len(smalls), len(outs), len(parts_of)

    def kernel(*refs):
        refs = list(refs)
        take = lambda n: [refs.pop(0) for _ in range(n)]
        in_refs, small_refs, out_refs = take(n_in), take(n_small), take(n_out)
        in_v, small_v, out_v = take(n_in), take(n_small), take(n_part)
        in_sems, small_sems, out_sems = refs

        def fetch(n, c):
            return pltpu.make_async_copy(window(in_refs[n], c), in_v[n].at[c], in_sems.at[n, c])

        def store(n, c):
            index, rows = parts_of[n]
            return pltpu.make_async_copy(out_v[n].at[c], window(out_refs[index], c, rows), out_sems.at[n, c])

        smalls_in = [pltpu.make_async_copy(small_refs[n], small_v[n], small_sems.at[n]) for n in range(n_small)]
        for copy in smalls_in:
            copy.start()
        for c in range(chunks):
            for n in range(n_in):
                fetch(n, c).start(priority=(n + c) % 2)
        for copy in smalls_in:
            copy.wait()

        @pl.loop(0, chunks)
        def _(c):
            for n in range(n_in):
                fetch(n, c).wait()
            body(c, [v.at[c] for v in in_v], small_v, [v.at[c] for v in out_v])
            for n in range(n_part):
                store(n, c).start()

        for c in range(chunks):
            for n in range(n_part):
                store(n, c).wait()

    scratch = [pltpu.VMEM((chunks,) + size(a.shape), a.dtype) for a in ins]
    scratch += [pltpu.VMEM(a.shape, a.dtype) for a in smalls]
    for index, rows in parts_of:
        shape = size(outs[index].shape)
        if rows is not None:
            shape = (shape[0], rows[1], shape[2])
        scratch.append(pltpu.VMEM((chunks,) + shape, outs[index].dtype))
    scratch += [pltpu.SemaphoreType.DMA((n_in, chunks)), pltpu.SemaphoreType.DMA((max(n_small, 1),)), pltpu.SemaphoreType.DMA((n_part, chunks))]
    total = sum(math.prod(a.shape) * a.dtype.itemsize for a in list(ins) + list(outs))
    anywhere = pl.BlockSpec(memory_space=pl.ANY)
    return pl.pallas_call(
        kernel,
        in_specs=[anywhere] * (n_in + n_small),
        out_specs=[anywhere] * n_out,
        out_shape=outs,
        scratch_shapes=scratch,
        compiler_params=pltpu.CompilerParams(vmem_limit_bytes=limit * MIB),
        cost_estimate=pl.CostEstimate(flops=total, bytes_accessed=total, transcendentals=0),
        name=name,
    )(*ins, *smalls)


def columns_of(ref, c, lanes):
    return ref[:, pl.ds(pl.multiple_of(c * lanes, 128), lanes)]


def short(taps, x0, x1, x2):
    return taps[0:1] * x0 + taps[1:2] * x1 + taps[2:3] * x2


def pack_body(c, ins, smalls, outs):
    cot, gate, filt, key, value = ins
    out = outs[0]
    rows, lanes = cot.shape
    mid = rows // 2
    kt, vt = (columns_of(x, c, lanes) for x in smalls)
    none = jnp.zeros((2, lanes), F32)
    edges, shorts = [[], []], []
    for x, taps in ((key, kt), (value, vt)):
        x = x[...].astype(F32)
        shorts.append(short(taps, x, *delayed(x, none)))
        last, prior = x[rows - 1 : rows], x[rows - 2 : rows - 1]
        edges[0].append(shorts[-1][0:2])
        edges[1] += [taps[1:2] * last + taps[2:3] * prior, taps[2:3] * last]
    edge = jnp.concatenate(edges[0] + edges[1], axis=0)
    coarse = edge.astype(BF).astype(F32)
    edge = jnp.concatenate([coarse, edge - coarse], axis=0)
    grad = cot[...].astype(F32) * gate[...].astype(F32)
    for n, x in enumerate((filt[...], shorts[0] * shorts[1], grad)):
        x = x.astype(BF)
        for j in range(lanes // 128):
            for h in range(2):
                turned = x[mid * h : mid * h + mid, 128 * j : 128 * j + 128].T
                at = 3 * HALF * h + HALF * n
                out[2 * j, at : at + HALF] = turned[:HALF]
                out[2 * j + 1, at : at + HALF] = turned[HALF:]
    for j in range(lanes // 128):
        tile = edge[:, 128 * j : 128 * j + 128]
        out[2 * j, 6 * HALF :] = tile.astype(BF)
        out[2 * j + 1, 6 * HALF :] = swap_halves(tile).astype(BF)


def gate_body(c, ins, smalls, outs):
    cot, conv = ins
    outs[0][...] = (cot[...].astype(F32) * conv[...].astype(F32)).astype(BF)


def turn_in(blocks):
    tiles = []
    for j in range(blocks.shape[0] // 2):
        pair = (blocks[2 * j], blocks[2 * j + 1])
        halves = [jnp.concatenate([x[at : at + HALF] for x in pair], axis=0).T for at in (0, HALF)]
        tiles.append(jnp.concatenate(halves, axis=0))
    return jnp.concatenate(tiles, axis=1).astype(F32)


def taps_body(c, ins, smalls, outs):
    grads, key, value = ins
    gz = turn_in(grads)
    kf, vf = key[...].astype(F32), value[...].astype(F32)
    kt, vt, before = (columns_of(x, c, kf.shape[1]).astype(F32) for x in smalls)
    ks, vs = (kf,) + delayed(kf, before[0:2]), (vf,) + delayed(vf, before[2:4])
    grad_key, grad_value = gz * short(vt, *vs), gz * short(kt, *ks)
    sums = [jnp.sum(grad_key * x, axis=0, keepdims=True) for x in ks]
    sums += [jnp.sum(grad_value * x, axis=0, keepdims=True) for x in vs]
    outs[0][...] = jnp.concatenate(sums + [jnp.zeros((2, kf.shape[1]), F32)], axis=0)


def inputs_body(c, ins, smalls, outs):
    grads, key, value = ins
    rows, lanes = key.shape
    gz = turn_in(grads)
    kf, vf = key[...].astype(F32), value[...].astype(F32)
    kt, vt, before, after = (columns_of(x, c, lanes).astype(F32) for x in smalls)
    edges = []
    for j in range(lanes // 128):
        edge = [grads[2 * j + n, 2 * HALF : 2 * HALF + 16, :].astype(F32) for n in range(2)]
        edges.append(jnp.where(low_lanes((16, 128)), edge[0], swap_halves(edge[1])))
    edge = jnp.concatenate(edges, axis=1)
    next0, next1 = edge[0:1], edge[1:2]

    def beyond(taps, x, edge):
        last, prior = x[rows - 1 : rows], x[rows - 2 : rows - 1]
        return short(taps, edge[0:1], last, prior), short(taps, edge[1:2], edge[0:1], last)

    def backward(taps, grad, grad0, grad1):
        one = with_bottom(pltpu.roll(grad, rows - 1, axis=0), [grad0])
        two = with_bottom(pltpu.roll(grad, rows - 2, axis=0), [grad0, grad1])
        return short(taps, grad, one, two)

    key_short, value_short = short(kt, kf, *delayed(kf, before[0:2])), short(vt, vf, *delayed(vf, before[2:4]))
    key_a, key_b = beyond(kt, kf, after[0:2])
    value_a, value_b = beyond(vt, vf, after[2:4])
    outs[0][...] = backward(kt, gz * value_short, next0 * value_a, next1 * value_b).astype(BF)
    outs[1][...] = backward(vt, gz * key_short, next0 * key_a, next1 * key_b).astype(BF)


def clip_body(c, ins, smalls, outs):
    outs[0][...] = turn_in(ins[0]) * smalls[0][0:1, 0:1]


def tree_step(x, axis, step):
    return x + lax.ppermute(x, axis, [(i, i ^ step) for i in range(lax.axis_size(axis))])


def quarter_sum(x, axis):
    size = lax.axis_size(axis)
    one, two, three = (lax.ppermute(x, axis, [(i, (i + n * size // 4) % size) for i in range(size)]) for n in (1, 2, 3))
    return (x + two) + (one + three)


def shards(gate_in, key_in, value_in, conv_out, cotangent, long_filter, key_taps, value_taps, *, parts, others):
    rows, columns = key_in.shape
    shape = jax.ShapeDtypeStruct
    block = shape((rows, columns), BF)
    tails = jnp.concatenate([key_in[-2:], value_in[-2:]], axis=0)
    heads = jnp.concatenate([key_in[:2], value_in[:2]], axis=0)
    (send,) = stream(
        pack_body,
        "pack",
        (cotangent, gate_in, long_filter, key_in, value_in),
        (key_taps, value_taps),
        (shape((parts, 6 * HALF + 16, rows // 2), BF),),
        ((0, None),),
        4,
        60,
    )
    recv = lax.all_to_all(send, "seq", 0, 0)
    send, tails, heads = lax.optimization_barrier((send, tails, heads))
    before = lax.ppermute(tails, "seq", [(i, i + 1) for i in range(parts - 1)])
    after = lax.ppermute(heads, "seq", [(i + 1, i) for i in range(parts - 1)])
    (gate_grad,) = stream(gate_body, "gate", (cotangent, conv_out), (), (block,), ((0, None),), 4, 16)
    recv, gate_grad = lax.optimization_barrier((recv, gate_grad))
    gz_send, gh_send = spectral(recv, parts, rows)
    gz_send, before, after = lax.optimization_barrier((gz_send, before, after))
    gz_recv = lax.all_to_all(gz_send, "seq", 0, 0)
    gz_recv, gh_send = lax.optimization_barrier((gz_recv, gh_send))
    gh_recv = lax.all_to_all(gh_send, "seq", 0, 0)
    (taps,) = stream(
        taps_body,
        "taps",
        (gz_recv, key_in, value_in),
        (key_taps, value_taps, before),
        (shape((8, columns), F32),),
        ((0, None),),
        4,
        LATE_LIMIT,
    )
    late, taps = lax.optimization_barrier((gz_recv, taps))
    total = jnp.sum(late[:, 2 * HALF + 2 : 2 * HALF + 4, :].astype(F32), axis=(0, 1))
    total = jnp.broadcast_to(total[None], (8, total.shape[0]))
    taps = tree_step(taps, "seq", 1)
    late, taps = lax.optimization_barrier((late, taps))
    key_grad, value_grad = stream(
        inputs_body,
        "inputs",
        (late, key_in, value_in),
        (key_taps, value_taps, before, after),
        (block, block),
        ((0, None), (1, None)),
        4,
        LATE_LIMIT,
    )
    taps = quarter_sum(taps, "seq")
    total = tree_step(total, "chan", 1)
    taps, total, key_grad, value_grad = lax.optimization_barrier((taps, total, key_grad, value_grad))
    total = tree_step(total, "chan", 3)
    taps = tree_step(taps, "seq", 2)
    count = rows * columns * parts * others
    scale = jnp.minimum(1.0, 1.0 / jnp.sqrt(total / count + 1e-6))
    taps, gh_recv = lax.optimization_barrier((taps, gh_recv))
    taps = tree_step(taps, "seq", 6)
    (filter_grad,) = stream(
        clip_body, "clip", (gh_recv,), (scale,), (shape((rows, columns), F32),), ((0, None),), 4, LATE_LIMIT
    )
    return (gate_grad, key_grad, value_grad, filter_grad, taps[0:3], taps[3:6])


def solution(mesh):
    blocks, vectors = P("seq", "chan"), P(None, "chan")
    return jax.shard_map(
        functools.partial(shards, parts=mesh.shape["seq"], others=mesh.shape["chan"]),
        mesh=mesh,
        in_specs=(blocks,) * 6 + (vectors,) * 2,
        out_specs=(blocks,) * 4 + (vectors,) * 2,
        check_vma=False,
    )
```

```python
import functools
import math

import jax
import jax.numpy as jnp
import numpy as np
from jax import lax
from jax.experimental import pallas as pl
from jax.experimental.pallas import tpu as pltpu
from jax.sharding import PartitionSpec as P

BF = jnp.bfloat16
F32 = jnp.float32
HALF = 64
MIB = 1 << 20
SPECTRAL_LIMIT = 60
LATE_LIMIT = 24


def transform_tables(parts, rows):
    length = parts * rows
    mid = rows // 2
    p = np.arange(parts)
    k = np.arange(parts)
    step = math.pi / (2 * length)
    angle = ((rows * p[None, :] * (4 * k[:, None] + 1)) % (4 * length)) * step
    first = np.stack([np.cos(angle), -np.sin(angle)], 1)
    forward = np.einsum("kcp,rs->kcrps", first, np.eye(8)).reshape(parts * 16, parts * 8)
    backward = forward.T / length
    angle = ((np.arange(rows)[None, :] * (4 * k[:, None] + 1)) % (4 * length)) * step
    factors = np.stack([np.cos(angle), np.sin(angle)], 1).astype(np.float32)
    r, j = np.arange(mid)[:, None], np.arange(mid)[None, :]
    second = []
    for odd in (0, 1):
        turn = (((2 * j + odd) * r) % rows) * (2 * math.pi / rows)
        cos, sin = np.cos(turn), np.sin(turn)
        second.append(np.block([[cos, -sin], [sin, cos]]))
    as_bf = lambda x: x.astype(np.float32).astype(jnp.bfloat16)
    second = np.stack(second)
    return as_bf(forward), as_bf(second), as_bf(second.transpose(0, 2, 1)), as_bf(backward), factors


def low_lanes(shape):
    return (lax.broadcasted_iota(jnp.int32, shape, len(shape) - 1) % 128) < HALF


def swap_halves(x):
    return pltpu.roll(x, HALF, axis=x.ndim - 1)


def spectral_kernel(recv, *refs):
    tables, (gz_out, gh_out), scratch = refs[:5], refs[5:7], refs[7:]
    m1, w, wi, m2, factors, x_v, gz_v, gh_v, y, u, in_sems, table_sems, out_sems = scratch
    parts, mid = recv.shape[0], recv.shape[2]
    rows = 2 * mid
    chans = (recv.shape[1] - 16) // 6
    group = parts
    pieces = 3

    def fetch(row, count, n):
        at = pl.ds(row, count)
        return pltpu.make_async_copy(recv.at[:, at, :], x_v.at[:, at, :], in_sems.at[n])

    def fetches(i):
        return [fetch(pl.multiple_of(3 * chans * h + chans * i, 16), chans, 2 * i + h) for h in range(2)]

    edges_in = fetch(6 * chans, 16, 2 * pieces)
    mixed_in, others_in = fetches(1), fetches(2) + fetches(0)
    tables_in = [pltpu.make_async_copy(tables[n], scratch[n], table_sems.at[n]) for n in range(5)]
    for copy in [edges_in] + mixed_in + [tables_in[0], tables_in[4]] + others_in + tables_in[1:4]:
        copy.start()

    for copy in [edges_in] + mixed_in:
        copy.wait()
    edges = x_v[:, 6 * chans : 6 * chans + 16, :].astype(F32)
    edges = edges[:, :8] + edges[:, 8:]
    ahead = jnp.concatenate([jnp.zeros((1, 8, 128), F32), edges[:-1]], axis=0)
    shorts = edges + pltpu.roll(ahead, 4, axis=1)
    starts = shorts * pltpu.roll(shorts, 6, axis=1)
    lane = lax.broadcasted_iota(jnp.int32, (chans, mid), 1)
    for p in range(parts):
        if p % 16 == 0:
            turned = starts[p : p + 16].reshape(128, 128).T[:chans]
        here = pltpu.roll(turned, (128 - 8 * (p % 16)) % 128, axis=1)
        old = x_v[p, chans : 2 * chans, :].astype(F32)
        x_v[p, chans : 2 * chans, :] = jnp.where(lane < 2, here, old).astype(BF)

    def forward(base):
        halves = [x_v[:, pl.ds(pl.multiple_of(3 * chans * h + base, 16), 16), :] for h in range(2)]
        x = jnp.concatenate(halves, axis=2).astype(F32)
        out = []
        for q in range(2):
            xq = x[:, 8 * q : 8 * q + 8, :].reshape(parts * 8, rows).astype(BF)
            out.append(jnp.dot(m1[...], xq, preferred_element_type=F32))
        for k in range(parts):
            c, s = factors[k, 0:1, :], factors[k, 1:2, :]
            sums, gaps = [], []
            for q in range(2):
                re, im = out[q][16 * k : 16 * k + 8], out[q][16 * k + 8 : 16 * k + 16]
                turned = (re * c + im * s, im * c - re * s)
                sums.append(jnp.concatenate([t[:, :mid] + t[:, mid:] for t in turned], axis=1))
                gaps.append(jnp.concatenate([t[:, :mid] - t[:, mid:] for t in turned], axis=1))
            y[0, k, pl.ds(base, 16), :] = jnp.concatenate(sums, axis=0).astype(BF)
            y[1, k, pl.ds(base, 16), :] = jnp.concatenate(gaps, axis=0).astype(BF)

    tables_in[0].wait()
    tables_in[4].wait()

    for i in (1, 2, 0):
        if i != 1:
            for copy in fetches(i):
                copy.wait()
        for q in range(chans // 16):
            forward(chans * i + 16 * q)

    tables_in[1].wait()
    tables_in[2].wait()

    @pl.loop(0, parts // group)
    def _(kk):
        backs = []
        for odd in range(2):
            lines = y[odd, pl.ds(group * kk, group)].reshape(group * 3 * chans, rows)
            spec = jnp.dot(lines, w[odd], preferred_element_type=F32)
            products = []
            for n in range(group):
                at = 3 * chans * n
                grad = spec[at + 2 * chans : at + 3 * chans]
                gr, gi = grad[:, :mid], grad[:, mid:]
                for h in range(2):
                    part = spec[at + h * chans : at + (h + 1) * chans]
                    sr, si = part[:, :mid], part[:, mid:]
                    products.append(jnp.concatenate([sr * gr + si * gi, sr * gi - si * gr], axis=1))
            product = jnp.concatenate(products, axis=0).astype(BF)
            backs.append(jnp.dot(product, wi[odd], preferred_element_type=F32))
        for h, back in enumerate((backs[0] + backs[1], backs[0] - backs[1])):
            cols = slice(mid * h, mid * h + mid)
            for n in range(group):
                k = group * kk + n
                c, s = factors[k, 0:1, cols], factors[k, 1:2, cols]
                lines = back[2 * chans * n : 2 * chans * (n + 1)]
                re, im = lines[:, :mid], lines[:, mid:]
                u[2 * k, :, cols] = (re * c - im * s).astype(BF)
                u[2 * k + 1, :, cols] = (im * c + re * s).astype(BF)

    def backward(base):
        piece = u[:, pl.ds(base, 16), :].astype(F32)
        outs = []
        for q in range(2):
            v = piece[:, 8 * q : 8 * q + 8, :].reshape(parts * 16, rows).astype(BF)
            out = jnp.dot(m2[...], v, preferred_element_type=F32)
            outs.append(out.reshape(parts, 8, rows))
        return jnp.concatenate(outs, axis=1)

    tiles = chans // 16

    def store(target, scratch, first, row):
        at = pl.ds(row, 16)
        return pltpu.make_async_copy(scratch.at[:, at, :], target.at[:, at, :], out_sems.at[first])

    tables_in[3].wait()
    for i in range(tiles):
        grad = backward(16 * i)
        for h in range(2):
            row = chans * h + 16 * i
            gz_v[:, row : row + 16, :] = grad[:, :, mid * h : mid * h + mid].astype(BF)
            store(gz_out, gz_v, 2 * tiles + tiles * h + i, row).start()

    for p in range(parts):
        after = jnp.zeros((16, 128), F32)
        if p + 1 < parts:
            at = (p + 1) // 2 * 2
            after = gz_v[at : at + 2, :chans, :].reshape(2 * chans, mid).T[:16].astype(F32)
            if (p + 1) % 2:
                after = swap_halves(after)
        gz_v[p, 2 * chans : 2 * chans + 16, :] = after.astype(BF)

    squares = jnp.zeros((8, rows), F32)
    for i in range(tiles):
        grad = backward(chans + 16 * i)
        for h in range(2):
            row = chans * h + 16 * i
            gh_v[:, row : row + 16, :] = grad[:, :, mid * h : mid * h + mid].astype(BF)
            store(gh_out, gh_v, tiles * h + i, row).start()
        squares += jnp.sum((grad * grad).reshape(parts * 2, 8, rows), axis=0)

    total = jnp.sum(jnp.sum(squares, axis=0, keepdims=True), axis=1, keepdims=True)
    coarse = total.astype(BF).astype(F32)
    fine = (total - coarse).astype(BF).astype(F32)
    row = lax.broadcasted_iota(jnp.int32, (16, 128), 0)
    sums = jnp.where(row == 2, coarse, jnp.where(row == 3, fine, 0.0))
    edges = gz_v[:, 2 * chans : 2 * chans + 16, :].astype(F32)
    gz_v[:, 2 * chans : 2 * chans + 16, :] = jnp.where(row[None] < 2, edges, sums[None]).astype(BF)
    store(gz_out, gz_v, 4 * tiles, 2 * chans).start()
    for n in range(2 * tiles):
        store(gh_out, gh_v, n, 16 * n).wait()
        store(gz_out, gz_v, 2 * tiles + n, 16 * n).wait()
    store(gz_out, gz_v, 4 * tiles, 2 * chans).wait()


def spectral(recv, parts, rows):
    tables = transform_tables(parts, rows)
    chans = (recv.shape[1] - 16) // 6
    mid = rows // 2
    anywhere = pl.BlockSpec(memory_space=pl.ANY)
    flops = 2 * parts * parts * 16 * 8 * rows * chans // 8 * 5 + 2 * parts * rows * rows * chans * 10
    return pl.pallas_call(
        spectral_kernel,
        out_shape=(
            jax.ShapeDtypeStruct((parts, 2 * chans + 16, mid), BF),
            jax.ShapeDtypeStruct((parts, 2 * chans, mid), BF),
        ),
        in_specs=[anywhere] * 6,
        out_specs=(anywhere, anywhere),
        scratch_shapes=[pltpu.VMEM(x.shape, x.dtype) for x in tables]
        + [
            pltpu.VMEM(recv.shape, BF),
            pltpu.VMEM((parts, 2 * chans + 16, mid), BF),
            pltpu.VMEM((parts, 2 * chans, mid), BF),
            pltpu.VMEM((2, parts, 3 * chans, rows), BF),
            pltpu.VMEM((2 * parts, 2 * chans, rows), BF),
            pltpu.SemaphoreType.DMA((7,)),
            pltpu.SemaphoreType.DMA((len(tables),)),
            pltpu.SemaphoreType.DMA((4 * (chans // 16) + 1,)),
        ],
        compiler_params=pltpu.CompilerParams(vmem_limit_bytes=SPECTRAL_LIMIT * MIB),
        cost_estimate=pl.CostEstimate(flops=flops, bytes_accessed=7 * MIB, transcendentals=0),
        name="spectral",
    )(recv, *[jnp.asarray(x) for x in tables])


def row_index(x):
    return lax.broadcasted_iota(jnp.int32, x.shape, 0)


def with_top(x, rows):
    top = x[:8]
    for n, line in enumerate(rows):
        top = jnp.where(row_index(top) == n, line, top)
    return jnp.concatenate([top, x[8:]], axis=0)


def with_bottom(x, rows):
    end = x.shape[0]
    bottom = x[end - 8 :]
    for n, line in enumerate(rows):
        bottom = jnp.where(row_index(bottom) == 8 - len(rows) + n, line, bottom)
    return jnp.concatenate([x[: end - 8], bottom], axis=0)


def delayed(x, before):
    first, second = before[0:1], before[1:2]
    one = with_top(pltpu.roll(x, 1, axis=0), [second])
    two = with_top(pltpu.roll(x, 2, axis=0), [first, second])
    return one, two


def stream(body, name, ins, smalls, outs, parts_of, chunks, limit):
    def size(shape):
        return (shape[0] // chunks,) + tuple(shape[1:]) if len(shape) == 3 else (shape[0], shape[1] // chunks)

    def window(ref, c, rows=None):
        if len(ref.shape) == 2:
            per = ref.shape[1] // chunks
            return ref.at[:, pl.ds(pl.multiple_of(c * per, 128), per)]
        per = ref.shape[0] // chunks
        at = ref.at[pl.ds(c * per, per)]
        return at if rows is None else ref.at[pl.ds(c * per, per), pl.ds(rows[0], rows[1]), :]

    n_in, n_small, n_out, n_part = len(ins), len(smalls), len(outs), len(parts_of)

    def kernel(*refs):
        refs = list(refs)
        take = lambda n: [refs.pop(0) for _ in range(n)]
        in_refs, small_refs, out_refs = take(n_in), take(n_small), take(n_out)
        in_v, small_v, out_v = take(n_in), take(n_small), take(n_part)
        in_sems, small_sems, out_sems = refs

        def fetch(n, c):
            return pltpu.make_async_copy(window(in_refs[n], c), in_v[n].at[c], in_sems.at[n, c])

        def store(n, c):
            index, rows = parts_of[n]
            return pltpu.make_async_copy(out_v[n].at[c], window(out_refs[index], c, rows), out_sems.at[n, c])

        smalls_in = [pltpu.make_async_copy(small_refs[n], small_v[n], small_sems.at[n]) for n in range(n_small)]
        for copy in smalls_in:
            copy.start()
        for c in range(chunks):
            for n in range(n_in):
                fetch(n, c).start(priority=(n + c) % 2)
        for copy in smalls_in:
            copy.wait()

        @pl.loop(0, chunks)
        def _(c):
            for n in range(n_in):
                fetch(n, c).wait()
            body(c, [v.at[c] for v in in_v], small_v, [v.at[c] for v in out_v])
            for n in range(n_part):
                store(n, c).start()

        for c in range(chunks):
            for n in range(n_part):
                store(n, c).wait()

    scratch = [pltpu.VMEM((chunks,) + size(a.shape), a.dtype) for a in ins]
    scratch += [pltpu.VMEM(a.shape, a.dtype) for a in smalls]
    for index, rows in parts_of:
        shape = size(outs[index].shape)
        if rows is not None:
            shape = (shape[0], rows[1], shape[2])
        scratch.append(pltpu.VMEM((chunks,) + shape, outs[index].dtype))
    scratch += [pltpu.SemaphoreType.DMA((n_in, chunks)), pltpu.SemaphoreType.DMA((max(n_small, 1),)), pltpu.SemaphoreType.DMA((n_part, chunks))]
    total = sum(math.prod(a.shape) * a.dtype.itemsize for a in list(ins) + list(outs))
    anywhere = pl.BlockSpec(memory_space=pl.ANY)
    return pl.pallas_call(
        kernel,
        in_specs=[anywhere] * (n_in + n_small),
        out_specs=[anywhere] * n_out,
        out_shape=outs,
        scratch_shapes=scratch,
        compiler_params=pltpu.CompilerParams(vmem_limit_bytes=limit * MIB),
        cost_estimate=pl.CostEstimate(flops=total, bytes_accessed=total, transcendentals=0),
        name=name,
    )(*ins, *smalls)


def columns_of(ref, c, lanes):
    return ref[:, pl.ds(pl.multiple_of(c * lanes, 128), lanes)]


def short(taps, x0, x1, x2):
    return taps[0:1] * x0 + taps[1:2] * x1 + taps[2:3] * x2


def pack_body(c, ins, smalls, outs):
    cot, gate, filt, key, value = ins
    out = outs[0]
    rows, lanes = cot.shape
    mid = rows // 2
    kt, vt = (columns_of(x, c, lanes) for x in smalls)
    none = jnp.zeros((2, lanes), F32)
    edges, shorts = [[], []], []
    for x, taps in ((key, kt), (value, vt)):
        x = x[...].astype(F32)
        shorts.append(short(taps, x, *delayed(x, none)))
        last, prior = x[rows - 1 : rows], x[rows - 2 : rows - 1]
        edges[0].append(shorts[-1][0:2])
        edges[1] += [taps[1:2] * last + taps[2:3] * prior, taps[2:3] * last]
    edge = jnp.concatenate(edges[0] + edges[1], axis=0)
    coarse = edge.astype(BF).astype(F32)
    edge = jnp.concatenate([coarse, edge - coarse], axis=0)
    grad = cot[...].astype(F32) * gate[...].astype(F32)
    for n, x in enumerate((filt[...], shorts[0] * shorts[1], grad)):
        x = x.astype(BF)
        for j in range(lanes // 128):
            for h in range(2):
                turned = x[mid * h : mid * h + mid, 128 * j : 128 * j + 128].T
                at = 3 * HALF * h + HALF * n
                out[2 * j, at : at + HALF] = turned[:HALF]
                out[2 * j + 1, at : at + HALF] = turned[HALF:]
    for j in range(lanes // 128):
        tile = edge[:, 128 * j : 128 * j + 128]
        out[2 * j, 6 * HALF :] = tile.astype(BF)
        out[2 * j + 1, 6 * HALF :] = swap_halves(tile).astype(BF)


def gate_body(c, ins, smalls, outs):
    cot, conv = ins
    outs[0][...] = (cot[...].astype(F32) * conv[...].astype(F32)).astype(BF)


def turn_in(blocks):
    tiles = []
    for j in range(blocks.shape[0] // 2):
        pair = (blocks[2 * j], blocks[2 * j + 1])
        halves = [jnp.concatenate([x[at : at + HALF] for x in pair], axis=0).T for at in (0, HALF)]
        tiles.append(jnp.concatenate(halves, axis=0))
    return jnp.concatenate(tiles, axis=1).astype(F32)


def taps_body(c, ins, smalls, outs):
    grads, key, value = ins
    gz = turn_in(grads)
    kf, vf = key[...].astype(F32), value[...].astype(F32)
    kt, vt, before = (columns_of(x, c, kf.shape[1]).astype(F32) for x in smalls)
    ks, vs = (kf,) + delayed(kf, before[0:2]), (vf,) + delayed(vf, before[2:4])
    grad_key, grad_value = gz * short(vt, *vs), gz * short(kt, *ks)
    sums = [jnp.sum(grad_key * x, axis=0, keepdims=True) for x in ks]
    sums += [jnp.sum(grad_value * x, axis=0, keepdims=True) for x in vs]
    outs[0][...] = jnp.concatenate(sums + [jnp.zeros((2, kf.shape[1]), F32)], axis=0)


def inputs_body(c, ins, smalls, outs):
    grads, key, value = ins
    rows, lanes = key.shape
    gz = turn_in(grads)
    kf, vf = key[...].astype(F32), value[...].astype(F32)
    kt, vt, before, after = (columns_of(x, c, lanes).astype(F32) for x in smalls)
    edges = []
    for j in range(lanes // 128):
        edge = [grads[2 * j + n, 2 * HALF : 2 * HALF + 16, :].astype(F32) for n in range(2)]
        edges.append(jnp.where(low_lanes((16, 128)), edge[0], swap_halves(edge[1])))
    edge = jnp.concatenate(edges, axis=1)
    next0, next1 = edge[0:1], edge[1:2]

    def beyond(taps, x, edge):
        last, prior = x[rows - 1 : rows], x[rows - 2 : rows - 1]
        return short(taps, edge[0:1], last, prior), short(taps, edge[1:2], edge[0:1], last)

    def backward(taps, grad, grad0, grad1):
        one = with_bottom(pltpu.roll(grad, rows - 1, axis=0), [grad0])
        two = with_bottom(pltpu.roll(grad, rows - 2, axis=0), [grad0, grad1])
        return short(taps, grad, one, two)

    key_short, value_short = short(kt, kf, *delayed(kf, before[0:2])), short(vt, vf, *delayed(vf, before[2:4]))
    key_a, key_b = beyond(kt, kf, after[0:2])
    value_a, value_b = beyond(vt, vf, after[2:4])
    outs[0][...] = backward(kt, gz * value_short, next0 * value_a, next1 * value_b).astype(BF)
    outs[1][...] = backward(vt, gz * key_short, next0 * key_a, next1 * key_b).astype(BF)


def clip_body(c, ins, smalls, outs):
    outs[0][...] = turn_in(ins[0]) * smalls[0][0:1, 0:1]


def tree_step(x, axis, step):
    return x + lax.ppermute(x, axis, [(i, i ^ step) for i in range(lax.axis_size(axis))])


def quarter_sum(x, axis):
    size = lax.axis_size(axis)
    one, two, three = (lax.ppermute(x, axis, [(i, (i + n * size // 4) % size) for i in range(size)]) for n in (1, 2, 3))
    return (x + two) + (one + three)


def shards(gate_in, key_in, value_in, conv_out, cotangent, long_filter, key_taps, value_taps, *, parts, others):
    rows, columns = key_in.shape
    shape = jax.ShapeDtypeStruct
    block = shape((rows, columns), BF)
    tails = jnp.concatenate([key_in[-2:], value_in[-2:]], axis=0)
    heads = jnp.concatenate([key_in[:2], value_in[:2]], axis=0)
    (send,) = stream(
        pack_body,
        "pack",
        (cotangent, gate_in, long_filter, key_in, value_in),
        (key_taps, value_taps),
        (shape((parts, 6 * HALF + 16, rows // 2), BF),),
        ((0, None),),
        4,
        60,
    )
    recv = lax.all_to_all(send, "seq", 0, 0)
    send, tails, heads = lax.optimization_barrier((send, tails, heads))
    before = lax.ppermute(tails, "seq", [(i, i + 1) for i in range(parts - 1)])
    after = lax.ppermute(heads, "seq", [(i + 1, i) for i in range(parts - 1)])
    (gate_grad,) = stream(gate_body, "gate", (cotangent, conv_out), (), (block,), ((0, None),), 4, 16)
    recv, gate_grad = lax.optimization_barrier((recv, gate_grad))
    gz_send, gh_send = spectral(recv, parts, rows)
    gz_send, before, after = lax.optimization_barrier((gz_send, before, after))
    gz_recv = lax.all_to_all(gz_send, "seq", 0, 0)
    gz_recv, gh_send = lax.optimization_barrier((gz_recv, gh_send))
    gh_recv = lax.all_to_all(gh_send, "seq", 0, 0)
    (taps,) = stream(
        taps_body,
        "taps",
        (gz_recv, key_in, value_in),
        (key_taps, value_taps, before),
        (shape((8, columns), F32),),
        ((0, None),),
        4,
        LATE_LIMIT,
    )
    late, taps = lax.optimization_barrier((gz_recv, taps))
    total = jnp.sum(late[:, 2 * HALF + 2 : 2 * HALF + 4, :].astype(F32), axis=(0, 1))
    total = jnp.broadcast_to(total[None], (8, total.shape[0]))
    taps = tree_step(taps, "seq", 1)
    late, taps = lax.optimization_barrier((late, taps))
    key_grad, value_grad = stream(
        inputs_body,
        "inputs",
        (late, key_in, value_in),
        (key_taps, value_taps, before, after),
        (block, block),
        ((0, None), (1, None)),
        4,
        LATE_LIMIT,
    )
    taps = quarter_sum(taps, "seq")
    total = tree_step(total, "chan", 1)
    taps, total, key_grad, value_grad = lax.optimization_barrier((taps, total, key_grad, value_grad))
    total = tree_step(total, "chan", 3)
    taps = tree_step(taps, "seq", 2)
    count = rows * columns * parts * others
    scale = jnp.minimum(1.0, 1.0 / jnp.sqrt(total / count + 1e-6))
    taps, gh_recv = lax.optimization_barrier((taps, gh_recv))
    taps = tree_step(taps, "seq", 6)
    (filter_grad,) = stream(
        clip_body, "clip", (gh_recv,), (scale,), (shape((rows, columns), F32),), ((0, None),), 4, LATE_LIMIT
    )
    return (gate_grad, key_grad, value_grad, filter_grad, taps[0:3], taps[3:6])


def solution(mesh):
    blocks, vectors = P("seq", "chan"), P(None, "chan")
    return jax.shard_map(
        functools.partial(shards, parts=mesh.shape["seq"], others=mesh.shape["chan"]),
        mesh=mesh,
        in_specs=(blocks,) * 6 + (vectors,) * 2,
        out_specs=(blocks,) * 4 + (vectors,) * 2,
        check_vma=False,
    )
```
